256 devices in a mesh: ctx: 32 (over z, x_lo, core), head: 8 (over y, x_hi).
Axes of the slice: x: 4 (x_hi: 2, x_lo: 2; x = x_hi * 2 + x_lo), y: 4, z: 8, core: 2. Of those that a mesh axis runs over, the one named last changes fastest.
Arguments:
- queries: bfloat16 [3, 64, 128, 192], P(None, 'ctx', 'head'), may hold values from -50 to 50, as said below
- cache: bfloat16 [32768, 576], P('ctx'), may hold values from -6 to 6
- w_uk: bfloat16 [128, 128, 512], P('head', 'ctx'), may hold values from -0.5 to 0.5
- w_uv: bfloat16 [128, 512, 128], P('head', 'ctx'), may hold values from -1 to 1
- selected: int32 [3, 64, 16], replicated, may hold values from 0 to 255, as said below
- lengths: int32 [64], replicated, may hold values from 2048 to 32766, as said below
Outputs:
- attended: bfloat16 [3, 64, 128, 128], P(None, 'ctx', 'head')
The draws below stay inside these ranges and needn't reach their ends.
Inputs may be any that keep to these rules, and one draw needn't show every extreme that they name: `queries`: in the shown draw of normal law; in the hidden draw some rows' rotary entries are large. `selected`: for each step and row, 16 distinct block numbers, block 0 among them, and each block b starts before the row's length (b * 128 < lengths[r]). `lengths`: both ends of the range are taken by some row in every draw.
All inputs are finite; a program needn't handle non-finite values.
Results may differ from the reference program's by a relative error of at most 0.0064.
Values may be sent and summed in bfloat16 or wider, within the bound.
No kernel may reach another device: no remote copies, remote signals or barrier semaphores. Data moves between devices by JAX's collectives and lax.ppermute only.
A program may use at most 64 MiB of HBM per device.

```python
import jax
import jax.numpy as jnp
from jax import lax

H = 128
DN = 128
R = 64
C = 512
DV = 128
BLK = 128
TOPK = 16
STEPS = 3
S_DEV = 1024
B = 64
CONTEXT = 32768
N_CTX = 32


def length_pattern(key):
    key = jax.random.fold_in(key, 101)
    key_main, key_pick = jax.random.split(key)
    lowest = TOPK * BLK
    highest = CONTEXT - STEPS + 1
    length_draw = jax.random.randint(key_main, (B,), lowest, highest + 1)
    shuffled = jax.random.permutation(key_pick, B)
    row_ids = jnp.arange(B)
    length_draw = jnp.where(row_ids == shuffled[0], highest, length_draw)
    length_draw = jnp.where(row_ids == shuffled[1], lowest, length_draw)
    return length_draw.astype(jnp.int32)


def draw_lengths(key, part):
    return length_pattern(key)


def draw_selected(key, part):
    length_draw = length_pattern(key)
    key = jax.random.fold_in(key, 7)
    block_total = CONTEXT // BLK
    blocks = jnp.arange(block_total, dtype=jnp.int32)
    random_scores = jax.random.randint(key, (STEPS, B, block_total), 0, 2 ** 20)
    ranked = random_scores * block_total + blocks
    allowed = blocks[None, None, :] * BLK < length_draw[None, :, None]
    ranked = jnp.where(allowed, ranked, -1 - blocks)
    ranked = jnp.where(blocks == 0, 2 ** 30, ranked)
    return lax.top_k(ranked, TOPK)[1].astype(jnp.int32)


def draw_queries(key, part):
    key = jax.random.fold_in(key, 11)
    full_shape = (STEPS, B, H, DN + R)
    values = jnp.clip(jax.random.normal(key, full_shape, jnp.float32), -6.0, 6.0)
    return values.astype(jnp.bfloat16)


def draw_cache(key, part):
    key = jax.random.fold_in(key, 23)
    key_main = jax.random.fold_in(key, 0)
    full_shape = (CONTEXT, C + R)
    values = jnp.clip(jax.random.normal(key_main, full_shape, jnp.float32), -6.0, 6.0)
    return values.astype(jnp.bfloat16)


def block_levels(stream_key, shape, cuts, least, top_value):
    loudness, own = 1.0, jax.random.fold_in(stream_key, 6)
    for dim, blocks in cuts:
        heights = jnp.exp(jax.random.uniform(jax.random.fold_in(own, dim), (blocks,), jnp.float32, least / len(cuts), top_value / len(cuts)))
        loudness = loudness * jnp.repeat(heights, shape[dim] // blocks).reshape([-1 if axis == dim else 1 for axis in range(len(shape))])
    return loudness


def gaussian(key, shape, deviation, most, cuts=(), held_as=jnp.bfloat16):
    entries = jax.random.normal(key, shape, jnp.float32) * deviation
    if len(cuts) > 0:
        entries = block_levels(key, shape, cuts, -0.22, 0.18) * entries
    return jnp.clip(entries, min=-most, max=most).astype(held_as)


def setup_inputs(seed: int = 0) -> dict:
    key_of = jax.random.split(jax.random.key(seed), 7)
    return {
        "queries": draw_queries(jax.random.fold_in(key_of[6], 71), 0),
        "cache": draw_cache(jax.random.fold_in(key_of[6], 71), 0),
        "w_uk": gaussian(key_of[2], (H, DN, C), DN ** -0.5, 0.5, ((0, 8), (1, 32))),
        "w_uv": gaussian(key_of[3], (H, C, DV), (C // 16) ** -0.5, 1.0, ((0, 8), (1, 32))),
        "selected": draw_selected(jax.random.fold_in(key_of[6], 71), 0),
        "lengths": draw_lengths(jax.random.fold_in(key_of[6], 71), 0),
    }


NEG_FILL = -1.0e30


def shard_terms(query_full, cache_rows, chosen_rows, length_rows, first_pos, step_index):
    scale_factor = (DN + R) ** -0.5
    shard_len = cache_rows.shape[0]
    scores = jnp.einsum("bhe,se->bhs", query_full.astype(jnp.float32), cache_rows.astype(jnp.float32)) * scale_factor
    positions = first_pos + jnp.arange(shard_len, dtype=jnp.int32)
    local_blocks = first_pos // BLK + jnp.arange(shard_len // BLK, dtype=jnp.int32)
    chosen_block = jnp.any(chosen_rows[:, :, None] == local_blocks[None, None, :], axis=1)
    chosen_token = jnp.broadcast_to(chosen_block[:, :, None], chosen_block.shape + (BLK,)).reshape(chosen_block.shape[0], shard_len)
    visible = (chosen_token & (positions[None, :] < length_rows[:, None] + step_index))[:, None, :]
    shard_max = jnp.max(jnp.where(visible, scores, NEG_FILL), axis=-1)
    weights = jnp.where(visible, jnp.exp(scores - shard_max[..., None]), 0.0).astype(jnp.bfloat16)
    shard_total = jnp.sum(weights.astype(jnp.float32), axis=-1)
    shard_latent = jnp.einsum("bhs,sc->bhc", weights.astype(jnp.float32), cache_rows[:, :C].astype(jnp.float32))
    return shard_max, shard_total, shard_latent


def reference(queries, cache, w_uk, w_uv, selected, lengths):
    results = []
    for step_index in range(STEPS):
        query_now = queries[step_index]
        absorbed = jnp.einsum("bhd,hdc->bhc", query_now[:, :, :DN].astype(jnp.float32), w_uk.astype(jnp.float32)).astype(jnp.bfloat16)
        query_full = jnp.concatenate([absorbed, query_now[:, :, DN:]], axis=-1)
        chosen_step = selected[step_index]

        def visit_shard(state_in, shard_index):
            running_max, running_total, running_latent = state_in
            first_pos = (shard_index * S_DEV).astype(jnp.int32)
            cache_rows = lax.dynamic_slice_in_dim(cache, first_pos, S_DEV, 0)
            shard_max, shard_total, shard_latent = shard_terms(query_full, cache_rows, chosen_step, lengths, first_pos, step_index)
            newest_max = jnp.maximum(running_max, shard_max)
            old_factor = jnp.exp(running_max - newest_max)
            new_factor = jnp.exp(shard_max - newest_max)
            running_total = running_total * old_factor + shard_total * new_factor
            running_latent = running_latent * old_factor[..., None] + shard_latent * new_factor[..., None]
            return (newest_max, running_total, running_latent), None

        initial = (jnp.full((B, H), NEG_FILL, jnp.float32), jnp.zeros((B, H), jnp.float32), jnp.zeros((B, H, C), jnp.float32))
        final_state, unused = lax.scan(visit_shard, initial, jnp.arange(N_CTX, dtype=jnp.int32))
        running_max, running_total, running_latent = final_state
        latent = running_latent / running_total[..., None]
        output = jnp.einsum("bhc,hcv->bhv", latent, w_uv.astype(jnp.float32), precision=lax.Precision.HIGHEST)
        results.append(output.astype(jnp.bfloat16))
    return jnp.stack(results, 0)
```

```python
import functools

import jax
import jax.numpy as jnp
from jax import lax
from jax.experimental import pallas as pl
from jax.experimental.pallas import tpu as pltpu
from jax.sharding import Mesh
from jax.sharding import PartitionSpec as P

DN = 128
R = 64
C = 512
DV = 128
BLK = 128
STEPS = 3

NZ = 8
NQ = 4
HG = 4
BZ = 8
RZ = STEPS * BZ
RT = NZ * RZ
S_DEV = 1024
NBLK = S_DEV // BLK

QN0, QR0, UK0, UV0, PIECE = 0, 96, 144, 400, 656
HALF = 320
OUT_ROWS = 112

NEG = -1e30
SCALE = (DN + R) ** (-0.5)
LOG2E = 1.4426950408889634
LN2 = 0.6931471805599453

VMEM = pl.BlockSpec(memory_space=pltpu.VMEM)
SMEM = pl.BlockSpec(memory_space=pltpu.SMEM)
ANY = pl.BlockSpec(memory_space=pl.ANY)


def dot(a, b, dims):
    return lax.dot_general(a, b, (dims, ((), ())), preferred_element_type=jnp.float32)


def attention_kernel(
    zsrc, *refs
):
    pieces = refs[:9]
    lim = refs[9]
    caches = refs[10:16]
    out = refs[16]
    cache, qn, qr, wuk, wuv, probe, scores, top, total, latent, sems = refs[17:]

    copies = []
    for i, (part, first, count) in enumerate(
        ((0, 0, 1024), (1, 0, 1024), (2, 0, 512), (2, 512, 512), (3, 0, 512), (3, 512, 512))
    ):
        copy = pltpu.make_async_copy(
            caches[i], cache.at[part, pl.ds(first, count), :], sems.at[i]
        )
        copy.start()
        copies.append(copy)

    for p in range(NZ):
        z = zsrc[p]

        def rows(first, count, p=p):
            if p < NZ - 1:
                return pieces[p][first : first + count, :]
            if first + count <= HALF:
                return pieces[p][first : first + count, :]
            return pieces[p + 1][first - HALF : first - HALF + count, :]

        here = pl.ds(pl.multiple_of(z * RZ, RZ), RZ)
        block = rows(QN0, 96).astype(jnp.float32)
        for h in range(HG):
            qn[h, here, :] = block[h * RZ : (h + 1) * RZ]
        block = rows(QR0, 48).astype(jnp.float32)
        for j in range(HG // 2):
            qr[j, here, :] = block[j * RZ : (j + 1) * RZ]
        here = pl.ds(pl.multiple_of(z * 16, 16), 16)
        for h in range(HG):
            for cc in range(4):
                wuk[h, here, cc * 128 : (cc + 1) * 128] = rows(UK0 + (h * 4 + cc) * 16, 16)
        for h in range(HG):
            here = pl.ds(pl.multiple_of(z * 64, 64), 64)
            wuv[h, here, :] = rows(UV0 + h * 64, 64)

    for h in range(HG):
        mine = slice(h * RT, (h + 1) * RT)
        absorbed = dot(qn[h].astype(jnp.bfloat16), wuk[h], ((1,), (0,)))
        probe[mine, 0:C] = absorbed.astype(jnp.bfloat16)
        rope = qr[h // 2][:, (h % 2) * R : (h % 2 + 1) * R]
        probe[mine, C : C + R] = rope.astype(jnp.bfloat16)
    top[...] = jnp.full(top.shape, NEG, jnp.float32)
    total[...] = jnp.zeros(total.shape, jnp.float32)
    latent[...] = jnp.zeros(latent.shape, jnp.float32)
    lane = lax.broadcasted_iota(jnp.int32, (RT, BLK), 1)

    for copy in copies:
        copy.wait()

    def score(i, carry):
        for h in range(HG):
            mine = pl.ds(h * RT, RT)
            part = dot(probe[mine, :], cache[i], ((1,), (1,)))
            best = top[mine, :]
            for j in range(NBLK):
                seen = lane < lim[i, :, j : j + 1]
                block = jnp.where(seen, part[:, j * BLK : (j + 1) * BLK], NEG)
                scores[i, mine, j * BLK : (j + 1) * BLK] = block
                best = jnp.maximum(best, block)
            top[mine, :] = best
        return carry

    lax.fori_loop(0, NQ, score, 0)

    best = jnp.max(top[...], axis=1, keepdims=True)
    top[...] = jnp.broadcast_to(best, top.shape)

    def weigh(i, carry):
        for h in range(HG):
            mine = pl.ds(h * RT, RT)
            best = jnp.maximum(top[mine, :], 0.1 * NEG)
            summed = total[mine, :]
            blocks = []
            for j in range(NBLK):
                block = scores[i, mine, j * BLK : (j + 1) * BLK]
                weight = jnp.exp2((block - best) * (SCALE * LOG2E))
                summed = summed + weight
                blocks.append(weight.astype(jnp.bfloat16))
            total[mine, :] = summed
            weights = jnp.concatenate(blocks, axis=1)
            latent[mine, :] += dot(weights, cache[i, :, 0:C], ((1,), (0,)))
        return carry

    lax.fori_loop(0, NQ, weigh, 0)

    parts, logs = [], []
    for h in range(HG):
        mine = slice(h * RT, (h + 1) * RT)
        norm = jnp.sum(total[mine, :], axis=1, keepdims=True)
        some = norm > 0.0
        norm = jnp.where(some, norm, 1.0)
        mean = (latent[mine, :] / norm).astype(jnp.bfloat16)
        parts.append(dot(mean, wuv[h], ((1,), (0,))))
        logs.append(jnp.where(some, top[mine, 0:1] * SCALE + jnp.log(norm), NEG))
    diagonal = lax.broadcasted_iota(jnp.int32, (96, 128), 0) == lax.broadcasted_iota(
        jnp.int32, (96, 128), 1
    )
    for z in range(NZ):
        rows = slice(z * RZ, (z + 1) * RZ)
        block = jnp.concatenate([part[rows] for part in parts], axis=0)
        out[z, 0:96, :] = block.astype(jnp.bfloat16)
        column = jnp.concatenate([log[rows] for log in logs], axis=0)
        row = jnp.sum(jnp.where(diagonal, column, 0.0), axis=0, keepdims=True)
        high = row.astype(jnp.bfloat16).astype(jnp.float32)
        middle = (row - high).astype(jnp.bfloat16).astype(jnp.float32)
        low = row - high - middle
        which = lax.broadcasted_iota(jnp.int32, (16, 128), 0)
        packed = jnp.where(
            which == 0, high, jnp.where(which == 1, middle, jnp.where(which == 2, low, 0.0))
        )
        out[z, 96:112, :] = packed.astype(jnp.bfloat16)


def attention(zsrc, pieces, lim, caches):
    return pl.pallas_call(
        attention_kernel,
        out_shape=jax.ShapeDtypeStruct((NZ, OUT_ROWS, 128), jnp.bfloat16),
        in_specs=[SMEM] + [VMEM] * 10 + [ANY] * 6,
        out_specs=VMEM,
        scratch_shapes=[
            pltpu.VMEM((NQ, S_DEV, C + R), jnp.bfloat16),
            pltpu.VMEM((HG, RT, DN), jnp.float32),
            pltpu.VMEM((HG // 2, RT, 2 * R), jnp.float32),
            pltpu.VMEM((HG, DN, C), jnp.bfloat16),
            pltpu.VMEM((HG, C, DV), jnp.bfloat16),
            pltpu.VMEM((HG * RT, C + R), jnp.bfloat16),
            pltpu.VMEM((NQ, HG * RT, S_DEV), jnp.float32),
            pltpu.VMEM((HG * RT, 128), jnp.float32),
            pltpu.VMEM((HG * RT, 128), jnp.float32),
            pltpu.VMEM((HG * RT, C), jnp.float32),
            pltpu.SemaphoreType.DMA((6,)),
        ],
        compiler_params=pltpu.CompilerParams(vmem_limit_bytes=48 * 1024 * 1024),
        cost_estimate=pl.CostEstimate(
            flops=2 * HG * RT * NQ * S_DEV * (2 * C + R),
            bytes_accessed=8 * 1024 * 1024,
            transcendentals=HG * RT * NQ * S_DEV,
        ),
        name="attention",
    )(zsrc, *pieces, lim, *caches)


def combine_kernel(parts, out):
    logs = []
    for z in range(NZ):
        packed = parts[z, 96:112, :].astype(jnp.float32)
        logs.append(packed[0:1] + packed[1:2] + packed[2:3])
    best = functools.reduce(jnp.maximum, logs)
    shares = [jnp.exp(log - best) for log in logs]
    norm = functools.reduce(jnp.add, shares)
    diagonal = lax.broadcasted_iota(jnp.int32, (96, 128), 0) == lax.broadcasted_iota(
        jnp.int32, (96, 128), 1
    )
    summed = jnp.zeros((96, 128), jnp.float32)
    for z in range(NZ):
        share = jnp.where(diagonal, shares[z] / norm, 0.0)
        column = jnp.sum(share, axis=1, keepdims=True)
        summed += column * parts[z, 0:96, :].astype(jnp.float32)
    out[...] = summed.astype(jnp.bfloat16)


def combine(parts):
    return pl.pallas_call(
        combine_kernel,
        out_shape=jax.ShapeDtypeStruct((96, 128), jnp.bfloat16),
        in_specs=[VMEM],
        out_specs=VMEM,
        name="combine",
    )(parts)


def quad_swap(x, k):
    return lax.ppermute(x, ("x", "core"), [(i, i ^ k) for i in range(NQ)])


def z_shift(x, k):
    return lax.ppermute(x, "z", [(i, (i + k) % NZ) for i in range(NZ)])


def quad_exchange(parts, quad):
    got = [lax.dynamic_index_in_dim(parts, quad, 0, keepdims=False)]
    for k in range(1, NQ):
        got.append(quad_swap(lax.dynamic_index_in_dim(parts, quad ^ k, 0, keepdims=False), k))
    odd = quad % 2 == 1
    a, b, c, d = got
    a, b, c, d = (
        jnp.where(odd, b, a),
        jnp.where(odd, a, b),
        jnp.where(odd, d, c),
        jnp.where(odd, c, d),
    )
    upper = quad >= 2
    return jnp.stack(
        [jnp.where(upper, c, a), jnp.where(upper, d, b), jnp.where(upper, a, c), jnp.where(upper, b, d)]
    )


def visible_limits(selected, lengths, z, quad):
    chosen = selected.reshape(STEPS, NZ, NQ, 2, -1).transpose(1, 2, 0, 3, 4).reshape(RT, -1)
    ends = lengths.reshape(NZ, NQ, 1, 2) + jnp.arange(STEPS, dtype=jnp.int32)[:, None]
    ends = ends.reshape(RT)
    first = (z * NQ + (quad ^ jnp.arange(NQ, dtype=jnp.int32))) * NBLK
    blocks = first[:, None] + jnp.arange(NBLK, dtype=jnp.int32)
    hit = jnp.any(chosen[None, :, None, :] == blocks[:, None, :, None], axis=-1)
    count = jnp.clip(ends[None, :, None] - blocks[:, None, :] * BLK, 0, BLK)
    return jnp.where(hit, count, 0)


def body(queries, cache, w_uk, w_uv, selected, lengths):
    z = lax.axis_index("z")
    quad = lax.axis_index("x") * 2 + lax.axis_index("core")

    q = queries.reshape(STEPS, 2, NQ, HG, DN + R)
    qn = q[..., :DN].transpose(2, 3, 0, 1, 4).reshape(NQ, 24, 128)
    qr = q[..., DN:].reshape(STEPS, 2, NQ, 2, 2, R).transpose(2, 3, 0, 1, 4, 5).reshape(NQ, 12, 128)
    uk = w_uk.reshape(NQ, HG, 4, 4, 128).transpose(0, 1, 3, 2, 4).reshape(NQ, 64, 128)
    uv = w_uv.reshape(NQ, 64, 128)
    got = quad_exchange(jnp.concatenate([qn, qr, uk, uv], axis=1), quad)
    piece = jnp.concatenate(
        [
            got[:, 0:24].reshape(NQ, HG, 6, 128).transpose(1, 0, 2, 3).reshape(96, 128),
            got[:, 24:36].reshape(NQ, 2, 6, 128).transpose(1, 0, 2, 3).reshape(48, 128),
            got[:, 36:100].reshape(NQ, 16, 4, 128).transpose(1, 0, 2, 3).reshape(256, 128),
            got[:, 100:164].reshape(NQ, HG, 16, 128).transpose(1, 0, 2, 3).reshape(256, 128),
        ],
        axis=0,
    )

    mate = quad_swap(cache, 1)
    low, high = quad_swap(cache[:512], 2), quad_swap(cache[512:], 2)
    caches = [cache, mate, low, high, quad_swap(low, 1), quad_swap(high, 1)]
    lim = visible_limits(selected, lengths, z, quad)

    up = down = piece
    pieces, offsets = [piece], [0]
    for step in range(1, 4):
        up, down = z_shift(up, 1), z_shift(down, -1)
        pieces += [up, down]
        offsets += [-step, step]
    pieces += [z_shift(up[:HALF], 1), z_shift(down[HALF:], -1)]
    offsets.append(4)
    zsrc = (z + jnp.array(offsets, jnp.int32)) % NZ

    parts = attention(zsrc, pieces, lim, caches)
    parts = lax.all_to_all(parts, "z", 0, 0, tiled=True)
    mine = combine(parts)
    mine = mine.reshape(HG, NQ, 6, 128).transpose(1, 0, 2, 3).reshape(NQ, 24, 128)
    final = quad_exchange(mine, quad)
    final = final.reshape(NQ, HG, STEPS, 2, DV).transpose(2, 3, 0, 1, 4)
    return final.reshape(STEPS, 2, NQ * HG, DV)


def solution(mesh):
    fine = Mesh(mesh.devices.reshape(NZ, 2, 2, -1), ("z", "x", "core", "head"))
    ctx = ("z", "x", "core")
    in_specs = (
        P(None, ctx, "head", None),
        P(ctx, None),
        P("head", ctx, None),
        P("head", ctx, None),
        P(),
        P(),
    )
    out_specs = P(None, ctx, "head", None)
    return jax.shard_map(body, mesh=fine, in_specs=in_specs, out_specs=out_specs, check_vma=False)
```

```python
import functools

import jax
import jax.numpy as jnp
from jax import lax
from jax.experimental import pallas as pl
from jax.experimental.pallas import tpu as pltpu
from jax.sharding import Mesh
from jax.sharding import PartitionSpec as P

DN = 128
R = 64
C = 512
DV = 128
BLK = 128
STEPS = 3
TOPK = 16

NZ = 8
NQ = 4
HG = 4
BZ = 8
RZ = STEPS * BZ
RT = NZ * RZ
RH = HG * RT
S_DEV = 1024
NBLK = S_DEV // BLK

QN0, QR0, UK0, UV0, PIECE = 0, 96, 144, 400, 656
HALF = 320
OFFSETS = (0, -1, 1, -2, 2, -3, 3, 4)
OUT_ROWS = 112

NEG = -1e30
SCALE = (DN + R) ** (-0.5)
LOG2E = 1.4426950408889634

VMEM = pl.BlockSpec(memory_space=pltpu.VMEM)


def dot(a, b, dims):
    return lax.dot_general(a, b, (dims, ((), ())), preferred_element_type=jnp.float32)


def iota(shape, dim):
    return lax.broadcasted_iota(jnp.int32, shape, dim)


def params():
    return pltpu.CompilerParams(vmem_limit_bytes=24 * 1024 * 1024)


def my_z():
    return lax.axis_index("z")


def my_quad():
    return lax.axis_index("x") * 2 + lax.axis_index("core")


def limits_kernel(chosen, lengths, out):
    z, quad = my_z(), my_quad()
    length = lengths[...]
    columns = [
        jnp.concatenate(
            [chosen[t], length >> 8, length & 255, jnp.zeros((14, 64), jnp.int32)], axis=0
        )
        for t in range(STEPS)
    ]
    table = jnp.concatenate(columns, axis=1).astype(jnp.float32).astype(jnp.bfloat16)
    row = iota((RT, RT), 0)
    row_z = (row * 2731) >> 16
    rest = row - row_z * RZ
    row_quad = (rest * 43) >> 8
    rest = rest - row_quad * 6
    source = (rest >> 1) * 64 + row_z * BZ + row_quad * 2 + (rest & 1)
    pick = jnp.where(source == iota((RT, RT), 1), 1.0, 0.0).astype(jnp.bfloat16)
    rows = dot(pick, table, ((1,), (1,))).astype(jnp.int32)
    row = iota((RT, 1), 0)
    within = row - ((row * 10923) >> 16) * 6
    ends = rows[:, 16:17] * 256 + rows[:, 17:18] + (within >> 1)
    lane = iota((RT, 128), 1)
    for i in range(NQ):
        block = (z * NQ + (quad ^ i)) * NBLK + lane
        hit = block == rows[:, 0:1]
        for k in range(1, TOPK):
            hit = jnp.logical_or(hit, block == rows[:, k : k + 1])
        count = jnp.clip(ends - block * BLK, 0, BLK)
        out[i] = jnp.where(hit, count, 0)


def visible_limits(selected, lengths):
    return pl.pallas_call(
        limits_kernel,
        out_shape=jax.ShapeDtypeStruct((NQ, RT, 128), jnp.int32),
        in_specs=[VMEM] * 2,
        out_specs=VMEM,
        name="limits",
    )(selected.transpose(0, 2, 1), lengths.reshape(1, -1))


def attend(parts, first, lim, probe, scores, top, total, latent):
    lane = iota((RT, BLK), 1)
    old = top[...]
    for i, part in enumerate(parts):
        whole = dot(probe[...], part[...], ((1,), (0,)))
        for h in range(HG):
            mine = slice(h * RT, (h + 1) * RT)
            best = top[mine, :]
            for j in range(NBLK):
                seen = lane < lim[first + i, :, j : j + 1]
                block = jnp.where(seen, whole[mine, j * BLK : (j + 1) * BLK], NEG)
                scores[i, mine, j * BLK : (j + 1) * BLK] = block
                best = jnp.maximum(best, block)
            top[mine, :] = best
    best = jnp.broadcast_to(jnp.max(top[...], axis=1, keepdims=True), top.shape)
    top[...] = best
    if first:
        fade = jnp.exp2((old - jnp.maximum(best, 0.1 * NEG)) * (SCALE * LOG2E))
        total[...] = total[...] * fade
        for c in range(C // 128):
            here = slice(c * 128, (c + 1) * 128)
            latent[:, here] = latent[:, here] * fade
    for i, part in enumerate(parts):
        weights = []
        for h in range(HG):
            mine = slice(h * RT, (h + 1) * RT)
            best = jnp.maximum(top[mine, :], 0.1 * NEG)
            summed = total[mine, :]
            blocks = []
            for j in range(NBLK):
                block = scores[i, mine, j * BLK : (j + 1) * BLK]
                weight = jnp.exp2((block - best) * (SCALE * LOG2E))
                summed = summed + weight
                blocks.append(weight.astype(jnp.bfloat16))
            total[mine, :] = summed
            weights.append(jnp.concatenate(blocks, axis=1))
        latent[...] += dot(jnp.concatenate(weights, axis=0), part[0:C, :], ((1,), (1,)))


def piece_rows(pieces, p, first, count):
    if p < NZ - 1 or first + count <= HALF:
        return pieces[p][first : first + count, :]
    return pieces[p + 1][first - HALF : first - HALF + count, :]


def near_kernel(*refs):
    pieces, (lim, own, mate), (probe, top, total, latent), (qn, qr, wuk, scores) = (
        refs[:9],
        refs[9:12],
        refs[12:16],
        refs[16:],
    )
    for p, offset in enumerate(OFFSETS):
        z = (my_z() + offset) & (NZ - 1)
        here = pl.ds(pl.multiple_of(z * RZ, RZ), RZ)
        block = piece_rows(pieces, p, QN0, 96).astype(jnp.float32)
        for h in range(HG):
            qn[h, here, :] = block[h * RZ : (h + 1) * RZ]
        block = piece_rows(pieces, p, QR0, 48).astype(jnp.float32)
        for j in range(HG // 2):
            qr[j, here, :] = block[j * RZ : (j + 1) * RZ]
        here = pl.ds(pl.multiple_of(z * 16, 16), 16)
        for h in range(HG):
            for cc in range(4):
                wuk[h, here, cc * 128 : (cc + 1) * 128] = piece_rows(
                    pieces, p, UK0 + (h * 4 + cc) * 16, 16
                )
    for h in range(HG):
        mine = slice(h * RT, (h + 1) * RT)
        absorbed = dot(qn[h].astype(jnp.bfloat16), wuk[h], ((1,), (0,)))
        probe[mine, 0:C] = absorbed.astype(jnp.bfloat16)
        rope = qr[h // 2][:, (h % 2) * R : (h % 2 + 1) * R]
        probe[mine, C : C + R] = rope.astype(jnp.bfloat16)
    top[...] = jnp.full(top.shape, NEG, jnp.float32)
    total[...] = jnp.zeros(total.shape, jnp.float32)
    latent[...] = jnp.zeros(latent.shape, jnp.float32)
    attend((own, mate), 0, lim, probe, scores, top, total, latent)


def near_positions(pieces, lim, own, mate):
    return pl.pallas_call(
        near_kernel,
        out_shape=(
            jax.ShapeDtypeStruct((RH, C + R), jnp.bfloat16),
            jax.ShapeDtypeStruct((RH, 128), jnp.float32),
            jax.ShapeDtypeStruct((RH, 128), jnp.float32),
            jax.ShapeDtypeStruct((RH, C), jnp.float32),
        ),
        in_specs=[VMEM] * 12,
        out_specs=(VMEM,) * 4,
        scratch_shapes=[
            pltpu.VMEM((HG, RT, DN), jnp.float32),
            pltpu.VMEM((HG // 2, RT, 2 * R), jnp.float32),
            pltpu.VMEM((HG, DN, C), jnp.bfloat16),
            pltpu.VMEM((2, RH, S_DEV), jnp.float32),
        ],
        compiler_params=params(),
        cost_estimate=pl.CostEstimate(
            flops=2 * RH * (2 * S_DEV * (2 * C + R) + DN * C),
            bytes_accessed=8 * 1024 * 1024,
            transcendentals=RH * 2 * S_DEV,
        ),
        name="near_positions",
    )(*pieces, lim, own, mate)


def middle_kernel(lim, low, probe, top_in, total_in, latent_in, top, total, latent, scores):
    top[...] = top_in[...]
    total[...] = total_in[...]
    latent[...] = latent_in[...]
    attend((low,), 2, lim, probe, scores, top, total, latent)


def middle_positions(lim, low, state):
    return pl.pallas_call(
        middle_kernel,
        out_shape=(
            jax.ShapeDtypeStruct((RH, 128), jnp.float32),
            jax.ShapeDtypeStruct((RH, 128), jnp.float32),
            jax.ShapeDtypeStruct((RH, C), jnp.float32),
        ),
        in_specs=[VMEM] * 6,
        out_specs=(VMEM,) * 3,
        scratch_shapes=[pltpu.VMEM((1, RH, S_DEV), jnp.float32)],
        compiler_params=params(),
        cost_estimate=pl.CostEstimate(
            flops=2 * RH * S_DEV * (2 * C + R),
            bytes_accessed=8 * 1024 * 1024,
            transcendentals=RH * S_DEV,
        ),
        name="middle_positions",
    )(lim, low, *state)


def far_kernel(*refs):
    pieces, (lim, high, probe, top_in, total_in, latent_in), out, (
        wuv,
        scores,
        top,
        total,
        latent,
    ) = refs[:9], refs[9:15], refs[15], refs[16:]
    for p, offset in enumerate(OFFSETS):
        z = (my_z() + offset) & (NZ - 1)
        here = pl.ds(pl.multiple_of(z * 64, 64), 64)
        for h in range(HG):
            wuv[h, here, :] = piece_rows(pieces, p, UV0 + h * 64, 64)
    top[...] = top_in[...]
    total[...] = total_in[...]
    latent[...] = latent_in[...]
    attend((high,), 3, lim, probe, scores, top, total, latent)

    parts, logs = [], []
    for h in range(HG):
        mine = slice(h * RT, (h + 1) * RT)
        norm = jnp.sum(total[mine, :], axis=1, keepdims=True)
        some = norm > 0.0
        norm = jnp.where(some, norm, 1.0)
        mean = (latent[mine, :] / norm).astype(jnp.bfloat16)
        parts.append(dot(mean, wuv[h], ((1,), (0,))))
        logs.append(jnp.where(some, top[mine, 0:1] * SCALE + jnp.log(norm), NEG))
    diagonal = iota((96, 128), 0) == iota((96, 128), 1)
    which = iota((16, 128), 0)
    for z in range(NZ):
        rows = slice(z * RZ, (z + 1) * RZ)
        block = jnp.concatenate([part[rows] for part in parts], axis=0)
        out[z, 0:96, :] = block.astype(jnp.bfloat16)
        column = jnp.concatenate([log[rows] for log in logs], axis=0)
        row = jnp.sum(jnp.where(diagonal, column, 0.0), axis=0, keepdims=True)
        high_part = row.astype(jnp.bfloat16).astype(jnp.float32)
        middle = (row - high_part).astype(jnp.bfloat16).astype(jnp.float32)
        rest = row - high_part - middle
        packed = jnp.where(
            which == 0,
            high_part,
            jnp.where(which == 1, middle, jnp.where(which == 2, rest, 0.0)),
        )
        out[z, 96:112, :] = packed.astype(jnp.bfloat16)


def far_positions(pieces, lim, high, state):
    return pl.pallas_call(
        far_kernel,
        out_shape=jax.ShapeDtypeStruct((NZ, OUT_ROWS, 128), jnp.bfloat16),
        in_specs=[VMEM] * 15,
        out_specs=VMEM,
        scratch_shapes=[
            pltpu.VMEM((HG, C, DV), jnp.bfloat16),
            pltpu.VMEM((1, RH, S_DEV), jnp.float32),
            pltpu.VMEM((RH, 128), jnp.float32),
            pltpu.VMEM((RH, 128), jnp.float32),
            pltpu.VMEM((RH, C), jnp.float32),
        ],
        compiler_params=params(),
        cost_estimate=pl.CostEstimate(
            flops=2 * RH * (S_DEV * (2 * C + R) + DV * C),
            bytes_accessed=8 * 1024 * 1024,
            transcendentals=RH * S_DEV,
        ),
        name="far_positions",
    )(*pieces, lim, high, *state)


def combine_kernel(parts, *outs):
    logs = []
    for z in range(NZ):
        packed = parts[z, 96:112, :].astype(jnp.float32)
        logs.append(packed[0:1] + packed[1:2] + packed[2:3])
    best = functools.reduce(jnp.maximum, logs)
    shares = [jnp.exp(log - best) for log in logs]
    norm = functools.reduce(jnp.add, shares)
    diagonal = iota((96, 128), 0) == iota((96, 128), 1)
    summed = jnp.zeros((96, 128), jnp.float32)
    for z in range(NZ):
        share = jnp.where(diagonal, shares[z] / norm, 0.0)
        column = jnp.sum(share, axis=1, keepdims=True)
        summed += column * parts[z, 0:96, :].astype(jnp.float32)
    row = iota((128, 96), 0)
    which, rest = row >> 5, row & 31
    head = (rest * 43) >> 8
    source = jnp.where(rest < 24, head * 24 + (my_quad() ^ which) * 6 + rest - head * 6, -1)
    pick = jnp.where(source == iota((128, 96), 1), 1.0, 0.0).astype(jnp.bfloat16)
    rows = dot(pick, summed.astype(jnp.bfloat16), ((1,), (0,))).astype(jnp.bfloat16)
    for k in range(NQ):
        outs[k][...] = rows[32 * k : 32 * (k + 1)]


def combine(parts):
    return pl.pallas_call(
        combine_kernel,
        out_shape=(jax.ShapeDtypeStruct((32, 128), jnp.bfloat16),) * NQ,
        in_specs=[VMEM],
        out_specs=(VMEM,) * NQ,
        name="combine",
    )(parts)


def quad_swap(x, k):
    return lax.ppermute(x, ("x", "core"), [(i, i ^ k) for i in range(NQ)])


def z_shift(x, k):
    return lax.ppermute(x, "z", [(i, (i + k) % NZ) for i in range(NZ)])


def by_sender(got):
    quad = my_quad()
    odd, upper = quad % 2 == 1, quad >= 2
    a, b, c, d = got
    a, b, c, d = (
        jnp.where(odd, b, a),
        jnp.where(odd, a, b),
        jnp.where(odd, d, c),
        jnp.where(odd, c, d),
    )
    return [
        jnp.where(upper, c, a),
        jnp.where(upper, d, b),
        jnp.where(upper, a, c),
        jnp.where(upper, b, d),
    ]


def quad_exchange(parts):
    quad = my_quad()
    got = [lax.dynamic_index_in_dim(parts, quad, 0, keepdims=False)]
    for k in range(1, NQ):
        got.append(quad_swap(lax.dynamic_index_in_dim(parts, quad ^ k, 0, keepdims=False), k))
    return jnp.stack(by_sender(got))


def body(queries, cache, w_uk, w_uv, selected, lengths):
    q = queries.reshape(STEPS, 2, NQ, HG, DN + R)
    qn = q[..., :DN].transpose(2, 3, 0, 1, 4).reshape(NQ, 24, 128)
    qr = q[..., DN:].reshape(STEPS, 2, NQ, 2, 2, R).transpose(2, 3, 0, 1, 4, 5).reshape(NQ, 12, 128)
    uk = w_uk.reshape(NQ, HG, 4, 4, 128).transpose(0, 1, 3, 2, 4).reshape(NQ, 64, 128)
    uv = w_uv.reshape(NQ, 64, 128)
    got = quad_exchange(jnp.concatenate([qn, qr, uk, uv], axis=1))
    piece = jnp.concatenate(
        [
            got[:, 0:24].reshape(NQ, HG, 6, 128).transpose(1, 0, 2, 3).reshape(96, 128),
            got[:, 24:36].reshape(NQ, 2, 6, 128).transpose(1, 0, 2, 3).reshape(48, 128),
            got[:, 36:100].reshape(NQ, 16, 4, 128).transpose(1, 0, 2, 3).reshape(256, 128),
            got[:, 100:164].reshape(NQ, HG, 16, 128).transpose(1, 0, 2, 3).reshape(256, 128),
        ],
        axis=0,
    )
    lim = visible_limits(selected, lengths)
    piece, lim, cache = lax.optimization_barrier((piece, lim, cache.T))

    up2, down2 = z_shift(piece, 2), z_shift(piece, -2)
    up1, down1 = z_shift(piece, 1), z_shift(piece, -1)
    mate, low = quad_swap(cache, 1), quad_swap(cache, 2)
    up2, down2, up1, down1, mate = lax.optimization_barrier((up2, down2, up1, down1, mate))
    up4, down4 = z_shift(up2[:HALF], 2), z_shift(down2[HALF:], -2)
    up3, down3 = z_shift(up2, 1), z_shift(down2, -1)
    pieces = [piece, up1, down1, up2, down2, up3, down3, up4, down4]

    probe, *state = near_positions(pieces, lim, cache, mate)
    low, probe, *state = lax.optimization_barrier((low, probe, *state))
    high = quad_swap(low, 1)
    state = middle_positions(lim, low, (probe, *state))
    parts = far_positions(pieces, lim, high, (probe, *state))
    parts = lax.all_to_all(parts, "z", 0, 0, tiled=True)
    mine = combine(parts)
    got = [mine[0]] + [quad_swap(mine[k], k) for k in range(1, NQ)]
    final = jnp.stack(by_sender(got))[:, :24]
    final = final.reshape(NQ, HG, STEPS, 2, DV).transpose(2, 3, 0, 1, 4)
    return final.reshape(STEPS, 2, NQ * HG, DV)


def solution(mesh):
    fine = Mesh(mesh.devices.reshape(NZ, 2, 2, -1), ("z", "x", "core", "head"))
    ctx = ("z", "x", "core")
    in_specs = (
        P(None, ctx, "head", None),
        P(ctx, None),
        P("head", ctx, None),
        P("head", ctx, None),
        P(),
        P(),
    )
    out_specs = P(None, ctx, "head", None)
    return jax.shard_map(body, mesh=fine, in_specs=in_specs, out_specs=out_specs, check_vma=False)
```

```python
import functools

import jax
import jax.numpy as jnp
from jax import lax
from jax.experimental import pallas as pl
from jax.experimental.pallas import tpu as pltpu
from jax.sharding import Mesh
from jax.sharding import PartitionSpec as P

DN = 128
R = 64
C = 512
DV = 128
BLK = 128
STEPS = 3
TOPK = 16

NZ = 8
NQ = 4
HG = 4
BZ = 8
RZ = STEPS * BZ
RT = NZ * RZ
RH = HG * RT
S_DEV = 1024
NBLK = S_DEV // BLK

QN0, QR0, UK0, UV0, PIECE = 0, 96, 144, 400, 656
OFFSETS = (0, -1, 1, -2, 2, -3, 3, 4)
EARLY = 5
OUT_ROWS = 112

NEG = -1e30
SCALE = (DN + R) ** (-0.5)
LOG2E = 1.4426950408889634

VMEM = pl.BlockSpec(memory_space=pltpu.VMEM)
HBM = pl.BlockSpec(memory_space=pltpu.HBM)


def dot(a, b, dims):
    return lax.dot_general(a, b, (dims, ((), ())), preferred_element_type=jnp.float32)


def iota(shape, dim):
    return lax.broadcasted_iota(jnp.int32, shape, dim)


def params():
    return pltpu.CompilerParams(vmem_limit_bytes=24 * 1024 * 1024)


def my_z():
    return lax.axis_index("z")


def my_quad():
    return lax.axis_index("x") * 2 + lax.axis_index("core")


def limits_kernel(chosen, lengths, out):
    z, quad = my_z(), my_quad()
    length = lengths[...]
    columns = [
        jnp.concatenate(
            [chosen[t], length >> 8, length & 255, jnp.zeros((14, 64), jnp.int32)], axis=0
        )
        for t in range(STEPS)
    ]
    table = jnp.concatenate(columns, axis=1).astype(jnp.float32).astype(jnp.bfloat16)
    row = iota((RT, RT), 0)
    row_z = (row * 2731) >> 16
    rest = row - row_z * RZ
    row_quad = (rest * 43) >> 8
    rest = rest - row_quad * 6
    source = (rest >> 1) * 64 + row_z * BZ + row_quad * 2 + (rest & 1)
    pick = jnp.where(source == iota((RT, RT), 1), 1.0, 0.0).astype(jnp.bfloat16)
    rows = dot(pick, table, ((1,), (1,))).astype(jnp.int32)
    row = iota((RT, 1), 0)
    within = row - ((row * 10923) >> 16) * 6
    ends = rows[:, 16:17] * 256 + rows[:, 17:18] + (within >> 1)
    lane = iota((RT, 128), 1)
    for i in range(NQ):
        block = (z * NQ + (quad ^ i)) * NBLK + lane
        hit = block == rows[:, 0:1]
        for k in range(1, TOPK):
            hit = jnp.logical_or(hit, block == rows[:, k : k + 1])
        count = jnp.clip(ends - block * BLK, 0, BLK)
        out[i] = jnp.where(hit, count, 0)


def visible_limits(selected, lengths):
    return pl.pallas_call(
        limits_kernel,
        out_shape=jax.ShapeDtypeStruct((NQ, RT, 128), jnp.int32),
        in_specs=[VMEM] * 2,
        out_specs=VMEM,
        name="limits",
    )(selected.transpose(0, 2, 1), lengths.reshape(1, -1))


def attend(parts, first, lim, probe, scores, top, total, latent, copies=()):
    lane = iota((RT, BLK), 1)
    old = top[...]
    for i, part in enumerate(parts):
        if i == len(parts) - 1:
            for copy in copies:
                copy.wait()
        whole = dot(probe[...], part[...], ((1,), (0,)))
        for h in range(HG):
            mine = slice(h * RT, (h + 1) * RT)
            best = top[mine, :]
            for j in range(NBLK):
                seen = lane < lim[first + i, :, j : j + 1]
                block = jnp.where(seen, whole[mine, j * BLK : (j + 1) * BLK], NEG)
                scores[i, mine, j * BLK : (j + 1) * BLK] = block
                best = jnp.maximum(best, block)
            top[mine, :] = best
    best = jnp.broadcast_to(jnp.max(top[...], axis=1, keepdims=True), top.shape)
    top[...] = best
    if first:
        fade = jnp.exp2((old - jnp.maximum(best, 0.1 * NEG)) * (SCALE * LOG2E))
        total[...] = total[...] * fade
        for c in range(C // 128):
            here = slice(c * 128, (c + 1) * 128)
            latent[:, here] = latent[:, here] * fade
    for i, part in enumerate(parts):
        weights = []
        for h in range(HG):
            mine = slice(h * RT, (h + 1) * RT)
            best = jnp.maximum(top[mine, :], 0.1 * NEG)
            summed = total[mine, :]
            blocks = []
            for j in range(NBLK):
                block = scores[i, mine, j * BLK : (j + 1) * BLK]
                weight = jnp.exp2((block - best) * (SCALE * LOG2E))
                summed = summed + weight
                blocks.append(weight.astype(jnp.bfloat16))
            total[mine, :] = summed
            weights.append(jnp.concatenate(blocks, axis=1))
        latent[...] += dot(jnp.concatenate(weights, axis=0), part[0:C, :], ((1,), (1,)))


def prepare_kernel(queries, keys, values, *refs):
    outs, (q, uk, uv, sems) = refs[:NQ], refs[NQ:]
    copies = [
        pltpu.make_async_copy(source, target, sems.at[i])
        for i, (source, target) in enumerate(((queries, q), (keys, uk), (values, uv)))
    ]
    for copy in copies:
        copy.start()
    quad = my_quad()
    row = iota((128, 96), 0)
    rest = row & 31
    head = (rest * 43) >> 8
    source = (rest - head * 6) * 16 + (quad ^ (row >> 5)) * HG + head
    source = jnp.where(rest < 24, source, -1)
    pick = jnp.where(source == iota((128, 96), 1), 1.0, 0.0).astype(jnp.bfloat16)
    row = iota((64, 96), 0)
    rest = row & 15
    pair = jnp.where(rest < 6, 0, 1)
    source = (rest - pair * 6) * 16 + (quad ^ (row >> 4)) * HG + pair * 2
    source = jnp.where(rest < 12, source, -1)
    column = iota((64, 96), 1)
    pick_even = jnp.where(source == column, 1.0, 0.0).astype(jnp.bfloat16)
    pick_odd = jnp.where(source == column - 1, 1.0, 0.0).astype(jnp.bfloat16)
    pick_odd = jnp.where(rest < 12, pick_odd, 0.0).astype(jnp.bfloat16)
    row = iota((64, 64), 0)
    source = (quad ^ (row >> 4)) * 16 + (row & 15)
    pick_keys = jnp.where(source == iota((64, 64), 1), 1.0, 0.0).astype(jnp.bfloat16)
    copies[0].wait()
    table = q[...].reshape(96, DN + R)
    plain = dot(pick, table[:, :DN], ((1,), (0,))).astype(jnp.bfloat16)
    rope = table[:, DN:]
    rope = jnp.concatenate(
        [dot(pick_even, rope, ((1,), (0,))), dot(pick_odd, rope, ((1,), (0,)))], axis=1
    ).astype(jnp.bfloat16)
    copies[1].wait()
    table = uk[...].astype(jnp.float32).reshape(64, C).astype(jnp.bfloat16)
    table = dot(pick_keys, table, ((1,), (0,))).astype(jnp.bfloat16)
    copies[2].wait()
    for k in range(NQ):
        for cc in range(4):
            outs[k][cc * 16 : (cc + 1) * 16, :] = table[
                k * 16 : (k + 1) * 16, cc * 128 : (cc + 1) * 128
            ]
        for h in range(HG):
            outs[k][64 + h * 16 : 80 + h * 16, :] = uv[(quad ^ k) * HG + h]
        outs[k][128:160, :] = plain[k * 32 : (k + 1) * 32]
        outs[k][160:176, :] = rope[k * 16 : (k + 1) * 16]


def prepare(queries, w_uk, w_uv):
    return pl.pallas_call(
        prepare_kernel,
        out_shape=(jax.ShapeDtypeStruct((176, 128), jnp.bfloat16),) * NQ,
        in_specs=[HBM] * 3,
        out_specs=(VMEM,) * NQ,
        scratch_shapes=[
            pltpu.VMEM((STEPS * 2, 16, DN + R), jnp.bfloat16),
            pltpu.VMEM((16, 4, C), jnp.bfloat16),
            pltpu.VMEM((16, 16, DV), jnp.bfloat16),
            pltpu.SemaphoreType.DMA((3,)),
        ],
        compiler_params=params(),
        name="prepare",
    )(queries.reshape(STEPS * 2, 16, DN + R), w_uk, w_uv)


def settle_kernel(*refs):
    arrived, mate_in, pieces, mate = refs[:EARLY], refs[EARLY], refs[EARLY + 1], refs[EARLY + 2]
    for p in range(EARLY):
        pieces[p] = arrived[p][...]
    mate[...] = mate_in[...]


def settle(arrived, mate):
    return pl.pallas_call(
        settle_kernel,
        out_shape=(
            jax.ShapeDtypeStruct((EARLY, PIECE, 128), jnp.bfloat16),
            jax.ShapeDtypeStruct(mate.shape, mate.dtype),
        ),
        in_specs=[VMEM] * (EARLY + 1),
        out_specs=(VMEM,) * 2,
        compiler_params=params(),
        name="settle",
    )(*arrived, mate)


def near_kernel(*refs):
    early, late, (lim, own, mate, low) = refs[0], refs[1:4], refs[4:8]
    probe, top, total, latent, qn, qr, wuk, scores, other, sem = refs[8:]
    copy = pltpu.make_async_copy(low, other, sem)
    copy.start()
    pieces = [early.at[p] for p in range(EARLY)] + list(late)
    for p, offset in enumerate(OFFSETS):
        z = (my_z() + offset) & (NZ - 1)
        here = pl.ds(pl.multiple_of(z * RZ, RZ), RZ)
        block = pieces[p][QN0 : QN0 + 96, :].astype(jnp.float32)
        for h in range(HG):
            qn[h, here, :] = block[h * RZ : (h + 1) * RZ]
        block = pieces[p][QR0 : QR0 + 48, :].astype(jnp.float32)
        for j in range(HG // 2):
            qr[j, here, :] = block[j * RZ : (j + 1) * RZ]
        here = pl.ds(pl.multiple_of(z * 16, 16), 16)
        for h in range(HG):
            for cc in range(4):
                first = UK0 + (cc * HG + h) * 16
                wuk[h, here, cc * 128 : (cc + 1) * 128] = pieces[p][first : first + 16, :]
    for h in range(HG):
        mine = slice(h * RT, (h + 1) * RT)
        absorbed = dot(qn[h].astype(jnp.bfloat16), wuk[h], ((1,), (0,)))
        probe[mine, 0:C] = absorbed.astype(jnp.bfloat16)
        rope = qr[h // 2][:, (h % 2) * R : (h % 2 + 1) * R]
        probe[mine, C : C + R] = rope.astype(jnp.bfloat16)
    top[...] = jnp.full(top.shape, NEG, jnp.float32)
    total[...] = jnp.zeros(total.shape, jnp.float32)
    latent[...] = jnp.zeros(latent.shape, jnp.float32)
    attend((own, mate, other), 0, lim, probe, scores, top, total, latent, (copy,))


def near_positions(pieces, lim, own, mate, low):
    return pl.pallas_call(
        near_kernel,
        out_shape=(
            jax.ShapeDtypeStruct((RH, C + R), jnp.bfloat16),
            jax.ShapeDtypeStruct((RH, 128), jnp.float32),
            jax.ShapeDtypeStruct((RH, 128), jnp.float32),
            jax.ShapeDtypeStruct((RH, C), jnp.float32),
        ),
        in_specs=[VMEM] * 7 + [HBM],
        out_specs=(VMEM,) * 4,
        scratch_shapes=[
            pltpu.VMEM((HG, RT, DN), jnp.float32),
            pltpu.VMEM((HG // 2, RT, 2 * R), jnp.float32),
            pltpu.VMEM((HG, DN, C), jnp.bfloat16),
            pltpu.VMEM((3, RH, S_DEV), jnp.float32),
            pltpu.VMEM((C + R, S_DEV), jnp.bfloat16),
            pltpu.SemaphoreType.DMA(()),
        ],
        compiler_params=params(),
        cost_estimate=pl.CostEstimate(
            flops=2 * RH * (3 * S_DEV * (2 * C + R) + DN * C),
            bytes_accessed=8 * 1024 * 1024,
            transcendentals=RH * 3 * S_DEV,
        ),
        name="near_positions",
    )(*pieces, lim, own, mate, low)


def far_kernel(*refs):
    early, late, (lim, high, probe, top_in, total_in, latent_in) = refs[0], refs[1:4], refs[4:10]
    out, wuv, scores, top, total, latent = refs[10:]
    pieces = [early.at[p] for p in range(EARLY)] + list(late)
    for p, offset in enumerate(OFFSETS):
        z = (my_z() + offset) & (NZ - 1)
        here = pl.ds(pl.multiple_of(z * 64, 64), 64)
        for h in range(HG):
            wuv[h, here, :] = pieces[p][UV0 + h * 64 : UV0 + (h + 1) * 64, :]
    top[...] = top_in[...]
    total[...] = total_in[...]
    latent[...] = latent_in[...]
    attend((high,), 3, lim, probe, scores, top, total, latent)

    parts, logs = [], []
    for h in range(HG):
        mine = slice(h * RT, (h + 1) * RT)
        norm = jnp.sum(total[mine, :], axis=1, keepdims=True)
        some = norm > 0.0
        norm = jnp.where(some, norm, 1.0)
        mean = (latent[mine, :] / norm).astype(jnp.bfloat16)
        parts.append(dot(mean, wuv[h], ((1,), (0,))))
        logs.append(jnp.where(some, top[mine, 0:1] * SCALE + jnp.log(norm), NEG))
    diagonal = iota((96, 128), 0) == iota((96, 128), 1)
    which = iota((16, 128), 0)
    for z in range(NZ):
        rows = slice(z * RZ, (z + 1) * RZ)
        block = jnp.concatenate([part[rows] for part in parts], axis=0)
        out[z, 0:96, :] = block.astype(jnp.bfloat16)
        column = jnp.concatenate([log[rows] for log in logs], axis=0)
        row = jnp.sum(jnp.where(diagonal, column, 0.0), axis=0, keepdims=True)
        high_part = row.astype(jnp.bfloat16).astype(jnp.float32)
        middle = (row - high_part).astype(jnp.bfloat16).astype(jnp.float32)
        rest = row - high_part - middle
        packed = jnp.where(
            which == 0,
            high_part,
            jnp.where(which == 1, middle, jnp.where(which == 2, rest, 0.0)),
        )
        out[z, 96:112, :] = packed.astype(jnp.bfloat16)


def far_positions(pieces, lim, high, state):
    return pl.pallas_call(
        far_kernel,
        out_shape=jax.ShapeDtypeStruct((NZ, OUT_ROWS, 128), jnp.bfloat16),
        in_specs=[VMEM] * 10,
        out_specs=VMEM,
        scratch_shapes=[
            pltpu.VMEM((HG, C, DV), jnp.bfloat16),
            pltpu.VMEM((1, RH, S_DEV), jnp.float32),
            pltpu.VMEM((RH, 128), jnp.float32),
            pltpu.VMEM((RH, 128), jnp.float32),
            pltpu.VMEM((RH, C), jnp.float32),
        ],
        compiler_params=params(),
        cost_estimate=pl.CostEstimate(
            flops=2 * RH * (S_DEV * (2 * C + R) + DV * C),
            bytes_accessed=8 * 1024 * 1024,
            transcendentals=RH * S_DEV,
        ),
        name="far_positions",
    )(*pieces, lim, high, *state)


def combine_kernel(parts, *outs):
    logs = []
    for z in range(NZ):
        packed = parts[z, 96:112, :].astype(jnp.float32)
        logs.append(packed[0:1] + packed[1:2] + packed[2:3])
    best = functools.reduce(jnp.maximum, logs)
    shares = [jnp.exp(log - best) for log in logs]
    norm = functools.reduce(jnp.add, shares)
    diagonal = iota((96, 128), 0) == iota((96, 128), 1)
    summed = jnp.zeros((96, 128), jnp.float32)
    for z in range(NZ):
        share = jnp.where(diagonal, shares[z] / norm, 0.0)
        column = jnp.sum(share, axis=1, keepdims=True)
        summed += column * parts[z, 0:96, :].astype(jnp.float32)
    row = iota((128, 96), 0)
    which, rest = row >> 5, row & 31
    head = (rest * 43) >> 8
    source = jnp.where(rest < 24, head * 24 + (my_quad() ^ which) * 6 + rest - head * 6, -1)
    pick = jnp.where(source == iota((128, 96), 1), 1.0, 0.0).astype(jnp.bfloat16)
    rows = dot(pick, summed.astype(jnp.bfloat16), ((1,), (0,))).astype(jnp.bfloat16)
    for k in range(NQ):
        outs[k][...] = rows[32 * k : 32 * (k + 1)]


def combine(parts):
    return pl.pallas_call(
        combine_kernel,
        out_shape=(jax.ShapeDtypeStruct((32, 128), jnp.bfloat16),) * NQ,
        in_specs=[VMEM],
        out_specs=(VMEM,) * NQ,
        name="combine",
    )(parts)


def quad_swap(x, k):
    return lax.ppermute(x, ("x", "core"), [(i, i ^ k) for i in range(NQ)])


def z_shift(x, k):
    return lax.ppermute(x, "z", [(i, (i + k) % NZ) for i in range(NZ)])


def opposite(up2, down2):
    core = lax.axis_index("core")
    pairs = [
        (2 * i + c, 2 * ((i + (2 if c == 0 else -2)) % NZ) + c) for i in range(NZ) for c in range(2)
    ]
    return lax.ppermute(jnp.where(core == 0, up2, down2), ("z", "core"), pairs)


def by_sender(got):
    quad = my_quad()
    odd, upper = quad % 2 == 1, quad >= 2
    a, b, c, d = got
    a, b, c, d = (
        jnp.where(odd, b, a),
        jnp.where(odd, a, b),
        jnp.where(odd, d, c),
        jnp.where(odd, c, d),
    )
    return [
        jnp.where(upper, c, a),
        jnp.where(upper, d, b),
        jnp.where(upper, a, c),
        jnp.where(upper, b, d),
    ]


def body(queries, cache, w_uk, w_uv, selected, lengths):
    sent = prepare(queries, w_uk, w_uv)
    got = jnp.stack(by_sender([sent[0]] + [quad_swap(sent[k], k) for k in range(1, NQ)]))
    piece = jnp.concatenate(
        [
            got[:, 128:152].reshape(NQ, HG, 6, 128).transpose(1, 0, 2, 3).reshape(96, 128),
            got[:, 160:172].reshape(NQ, 2, 6, 128).transpose(1, 0, 2, 3).reshape(48, 128),
            got[:, 0:64].reshape(NQ, 16, 4, 128).transpose(1, 0, 2, 3).reshape(256, 128),
            got[:, 64:128].reshape(NQ, HG, 16, 128).transpose(1, 0, 2, 3).reshape(256, 128),
        ],
        axis=0,
    )
    lim = visible_limits(selected, lengths)
    piece, lim, cache = lax.optimization_barrier((piece, lim, cache.T))
    low, mate = quad_swap(cache, 2), quad_swap(cache, 1)
    up1, down1 = z_shift(piece, 1), z_shift(piece, -1)
    up2, down2 = z_shift(piece, 2), z_shift(piece, -2)
    mate, up1, down1, up2, down2 = lax.optimization_barrier((mate, up1, down1, up2, down2))
    up3, down3 = z_shift(up2, 1), z_shift(down2, -1)
    late = [up3, down3, opposite(up2, down2)]
    early, mate = settle([piece, up1, down1, up2, down2], mate)

    low, late = lax.optimization_barrier((low, late))
    high = quad_swap(low, 1)
    probe, *state = near_positions([early] + late, lim, cache, mate, low)
    parts = far_positions([early] + late, lim, high, (probe, *state))
    parts = lax.all_to_all(parts, "z", 0, 0, tiled=True)
    mine = combine(parts)
    got = [mine[0]] + [quad_swap(mine[k], k) for k in range(1, NQ)]
    final = jnp.stack(by_sender(got))[:, :24]
    final = final.reshape(NQ, HG, STEPS, 2, DV).transpose(2, 3, 0, 1, 4)
    return final.reshape(STEPS, 2, NQ * HG, DV)


def solution(mesh):
    fine = Mesh(mesh.devices.reshape(NZ, 2, 2, -1), ("z", "x", "core", "head"))
    ctx = ("z", "x", "core")
    in_specs = (
        P(None, ctx, "head", None),
        P(ctx, None),
        P("head", ctx, None),
        P("head", ctx, None),
        P(),
        P(),
    )
    out_specs = P(None, ctx, "head", None)
    return jax.shard_map(body, mesh=fine, in_specs=in_specs, out_specs=out_specs, check_vma=False)
```

```python
import functools

import jax
import jax.numpy as jnp
from jax import lax
from jax.experimental import pallas as pl
from jax.experimental.pallas import tpu as pltpu
from jax.sharding import Mesh
from jax.sharding import PartitionSpec as P

DN = 128
R = 64
C = 512
DV = 128
BLK = 128
STEPS = 3
TOPK = 16

NZ = 8
NQ = 4
HG = 4
BZ = 8
RZ = STEPS * BZ
RT = NZ * RZ
RH = HG * RT
S_DEV = 1024
NBLK = S_DEV // BLK

QN0, QR0, UK0, UV0, PIECE = 0, 96, 144, 400, 656
OFFSETS = (0, -1, 1, -2, 2, -3, 3, 4)
EARLY = 5
OUT_ROWS = 112

NEG = -1e30
SCALE = (DN + R) ** (-0.5)
LOG2E = 1.4426950408889634

VMEM = pl.BlockSpec(memory_space=pltpu.VMEM)
HBM = pl.BlockSpec(memory_space=pltpu.HBM)


def dot(a, b, dims):
    return lax.dot_general(a, b, (dims, ((), ())), preferred_element_type=jnp.float32)


def iota(shape, dim):
    return lax.broadcasted_iota(jnp.int32, shape, dim)


def params(mebibytes=24):
    return pltpu.CompilerParams(vmem_limit_bytes=mebibytes * 1024 * 1024)


def my_z():
    return lax.axis_index("z")


def my_quad():
    return lax.axis_index("x") * 2 + lax.axis_index("core")


def limits_kernel(chosen, lengths, out):
    z, quad = my_z(), my_quad()
    length = lengths[...]
    columns = [
        jnp.concatenate(
            [chosen[t], length >> 8, length & 255, jnp.zeros((14, 64), jnp.int32)], axis=0
        )
        for t in range(STEPS)
    ]
    table = jnp.concatenate(columns, axis=1).astype(jnp.float32).astype(jnp.bfloat16)
    row = iota((RT, RT), 0)
    row_z = (row * 2731) >> 16
    rest = row - row_z * RZ
    row_quad = (rest * 43) >> 8
    rest = rest - row_quad * 6
    source = (rest >> 1) * 64 + row_z * BZ + row_quad * 2 + (rest & 1)
    pick = jnp.where(source == iota((RT, RT), 1), 1.0, 0.0).astype(jnp.bfloat16)
    rows = dot(pick, table, ((1,), (1,))).astype(jnp.int32)
    row = iota((RT, 1), 0)
    within = row - ((row * 10923) >> 16) * 6
    ends = rows[:, 16:17] * 256 + rows[:, 17:18] + (within >> 1)
    lane = iota((RT, 128), 1)
    for i in range(NQ):
        block = (z * NQ + (quad ^ i)) * NBLK + lane
        hit = block == rows[:, 0:1]
        for k in range(1, TOPK):
            hit = jnp.logical_or(hit, block == rows[:, k : k + 1])
        count = jnp.clip(ends - block * BLK, 0, BLK)
        out[i] = jnp.where(hit, count, 0)


def visible_limits(selected, lengths):
    return pl.pallas_call(
        limits_kernel,
        out_shape=jax.ShapeDtypeStruct((NQ, RT, 128), jnp.int32),
        in_specs=[VMEM] * 2,
        out_specs=VMEM,
        name="limits",
    )(selected.transpose(0, 2, 1), lengths.reshape(1, -1))


def attend(parts, first, lim, probe, scores, top, total, latent, copies=()):
    lane = iota((RT, BLK), 1)
    old = top[...]
    for i, part in enumerate(parts):
        if i == len(parts) - 1:
            for copy in copies:
                copy.wait()
        whole = dot(probe[...], part[...], ((1,), (0,)))
        for h in range(HG):
            mine = slice(h * RT, (h + 1) * RT)
            best = top[mine, :]
            for j in range(NBLK):
                seen = lane < lim[first + i, :, j : j + 1]
                block = jnp.where(seen, whole[mine, j * BLK : (j + 1) * BLK], NEG)
                scores[i, mine, j * BLK : (j + 1) * BLK] = block
                best = jnp.maximum(best, block)
            top[mine, :] = best
    best = jnp.broadcast_to(jnp.max(top[...], axis=1, keepdims=True), top.shape)
    top[...] = best
    if first:
        fade = jnp.exp2((old - jnp.maximum(best, 0.1 * NEG)) * (SCALE * LOG2E))
        total[...] = total[...] * fade
        for c in range(C // 128):
            here = slice(c * 128, (c + 1) * 128)
            latent[:, here] = latent[:, here] * fade
    for i, part in enumerate(parts):
        weights = []
        for h in range(HG):
            mine = slice(h * RT, (h + 1) * RT)
            best = jnp.maximum(top[mine, :], 0.1 * NEG)
            summed = total[mine, :]
            blocks = []
            for j in range(NBLK):
                block = scores[i, mine, j * BLK : (j + 1) * BLK]
                weight = jnp.exp2((block - best) * (SCALE * LOG2E))
                summed = summed + weight
                blocks.append(weight.astype(jnp.bfloat16))
            total[mine, :] = summed
            weights.append(jnp.concatenate(blocks, axis=1))
        latent[...] += dot(jnp.concatenate(weights, axis=0), part[0:C, :], ((1,), (1,)))


def prepare_kernel(queries, keys, values, *refs):
    outs, (q, uk, uv, sems) = refs[:NQ], refs[NQ:]
    copies = [
        pltpu.make_async_copy(source, target, sems.at[i])
        for i, (source, target) in enumerate(((queries, q), (keys, uk), (values, uv)))
    ]
    for copy in copies:
        copy.start()
    quad = my_quad()
    row = iota((128, 96), 0)
    rest = row & 31
    head = (rest * 43) >> 8
    source = (rest - head * 6) * 16 + (quad ^ (row >> 5)) * HG + head
    source = jnp.where(rest < 24, source, -1)
    pick = jnp.where(source == iota((128, 96), 1), 1.0, 0.0).astype(jnp.bfloat16)
    row = iota((64, 96), 0)
    rest = row & 15
    pair = jnp.where(rest < 6, 0, 1)
    source = (rest - pair * 6) * 16 + (quad ^ (row >> 4)) * HG + pair * 2
    source = jnp.where(rest < 12, source, -1)
    column = iota((64, 96), 1)
    pick_even = jnp.where(source == column, 1.0, 0.0).astype(jnp.bfloat16)
    pick_odd = jnp.where(source == column - 1, 1.0, 0.0).astype(jnp.bfloat16)
    pick_odd = jnp.where(rest < 12, pick_odd, 0.0).astype(jnp.bfloat16)
    row = iota((64, 64), 0)
    source = (quad ^ (row >> 4)) * 16 + (row & 15)
    pick_keys = jnp.where(source == iota((64, 64), 1), 1.0, 0.0).astype(jnp.bfloat16)
    copies[0].wait()
    table = q[...].reshape(96, DN + R)
    plain = dot(pick, table[:, :DN], ((1,), (0,))).astype(jnp.bfloat16)
    rope = table[:, DN:]
    rope = jnp.concatenate(
        [dot(pick_even, rope, ((1,), (0,))), dot(pick_odd, rope, ((1,), (0,)))], axis=1
    ).astype(jnp.bfloat16)
    copies[1].wait()
    table = uk[...].astype(jnp.float32).reshape(64, C).astype(jnp.bfloat16)
    table = dot(pick_keys, table, ((1,), (0,))).astype(jnp.bfloat16)
    copies[2].wait()
    for k in range(NQ):
        for cc in range(4):
            outs[k][cc * 16 : (cc + 1) * 16, :] = table[
                k * 16 : (k + 1) * 16, cc * 128 : (cc + 1) * 128
            ]
        for h in range(HG):
            outs[k][64 + h * 16 : 80 + h * 16, :] = uv[(quad ^ k) * HG + h]
        outs[k][128:160, :] = plain[k * 32 : (k + 1) * 32]
        outs[k][160:176, :] = rope[k * 16 : (k + 1) * 16]


def prepare(queries, w_uk, w_uv):
    return pl.pallas_call(
        prepare_kernel,
        out_shape=(jax.ShapeDtypeStruct((176, 128), jnp.bfloat16),) * NQ,
        in_specs=[HBM] * 3,
        out_specs=(VMEM,) * NQ,
        scratch_shapes=[
            pltpu.VMEM((STEPS * 2, 16, DN + R), jnp.bfloat16),
            pltpu.VMEM((16, 4, C), jnp.bfloat16),
            pltpu.VMEM((16, 16, DV), jnp.bfloat16),
            pltpu.SemaphoreType.DMA((3,)),
        ],
        compiler_params=params(8),
        name="prepare",
    )(queries.reshape(STEPS * 2, 16, DN + R), w_uk, w_uv)


def settle_kernel(*refs):
    arrived, mate_in, pieces, mate = refs[:EARLY], refs[EARLY], refs[EARLY + 1], refs[EARLY + 2]
    for p in range(EARLY):
        pieces[p] = arrived[p][...]
    mate[...] = mate_in[...]


def settle(arrived, mate):
    return pl.pallas_call(
        settle_kernel,
        out_shape=(
            jax.ShapeDtypeStruct((EARLY, PIECE, 128), jnp.bfloat16),
            jax.ShapeDtypeStruct(mate.shape, mate.dtype),
        ),
        in_specs=[VMEM] * (EARLY + 1),
        out_specs=(VMEM,) * 2,
        compiler_params=params(8),
        name="settle",
    )(*arrived, mate)


def near_kernel(*refs):
    early, late, (lim, own, mate, low) = refs[0], refs[1:4], refs[4:8]
    probe, top, total, latent, qn, qr, wuk, scores, other, sem = refs[8:]
    copy = pltpu.make_async_copy(low, other, sem)
    copy.start()
    pieces = [early.at[p] for p in range(EARLY)] + list(late)
    for p, offset in enumerate(OFFSETS):
        z = (my_z() + offset) & (NZ - 1)
        here = pl.ds(pl.multiple_of(z * RZ, RZ), RZ)
        block = pieces[p][QN0 : QN0 + 96, :].astype(jnp.float32)
        for h in range(HG):
            qn[h, here, :] = block[h * RZ : (h + 1) * RZ]
        block = pieces[p][QR0 : QR0 + 48, :].astype(jnp.float32)
        for j in range(HG // 2):
            qr[j, here, :] = block[j * RZ : (j + 1) * RZ]
        here = pl.ds(pl.multiple_of(z * 16, 16), 16)
        for h in range(HG):
            for cc in range(4):
                first = UK0 + (cc * HG + h) * 16
                wuk[h, here, cc * 128 : (cc + 1) * 128] = pieces[p][first : first + 16, :]
    for h in range(HG):
        mine = slice(h * RT, (h + 1) * RT)
        absorbed = dot(qn[h].astype(jnp.bfloat16), wuk[h], ((1,), (0,)))
        probe[mine, 0:C] = absorbed.astype(jnp.bfloat16)
        rope = qr[h // 2][:, (h % 2) * R : (h % 2 + 1) * R]
        probe[mine, C : C + R] = rope.astype(jnp.bfloat16)
    top[...] = jnp.full(top.shape, NEG, jnp.float32)
    total[...] = jnp.zeros(total.shape, jnp.float32)
    latent[...] = jnp.zeros(latent.shape, jnp.float32)
    attend((own, mate, other), 0, lim, probe, scores, top, total, latent, (copy,))


def near_positions(pieces, lim, own, mate, low):
    return pl.pallas_call(
        near_kernel,
        out_shape=(
            jax.ShapeDtypeStruct((RH, C + R), jnp.bfloat16),
            jax.ShapeDtypeStruct((RH, 128), jnp.float32),
            jax.ShapeDtypeStruct((RH, 128), jnp.float32),
            jax.ShapeDtypeStruct((RH, C), jnp.float32),
        ),
        in_specs=[VMEM] * 7 + [HBM],
        out_specs=(VMEM,) * 4,
        scratch_shapes=[
            pltpu.VMEM((HG, RT, DN), jnp.float32),
            pltpu.VMEM((HG // 2, RT, 2 * R), jnp.float32),
            pltpu.VMEM((HG, DN, C), jnp.bfloat16),
            pltpu.VMEM((3, RH, S_DEV), jnp.float32),
            pltpu.VMEM((C + R, S_DEV), jnp.bfloat16),
            pltpu.SemaphoreType.DMA(()),
        ],
        compiler_params=params(),
        cost_estimate=pl.CostEstimate(
            flops=2 * RH * (3 * S_DEV * (2 * C + R) + DN * C),
            bytes_accessed=8 * 1024 * 1024,
            transcendentals=RH * 3 * S_DEV,
        ),
        name="near_positions",
    )(*pieces, lim, own, mate, low)


def far_kernel(*refs):
    early, late, (lim, high, probe, top_in, total_in, latent_in) = refs[0], refs[1:4], refs[4:10]
    out, wuv, scores, top, total, latent = refs[10:]
    pieces = [early.at[p] for p in range(EARLY)] + list(late)
    for p, offset in enumerate(OFFSETS):
        z = (my_z() + offset) & (NZ - 1)
        here = pl.ds(pl.multiple_of(z * 64, 64), 64)
        for h in range(HG):
            wuv[h, here, :] = pieces[p][UV0 + h * 64 : UV0 + (h + 1) * 64, :]
    top[...] = top_in[...]
    total[...] = total_in[...]
    latent[...] = latent_in[...]
    attend((high,), 3, lim, probe, scores, top, total, latent)

    parts, logs = [], []
    for h in range(HG):
        mine = slice(h * RT, (h + 1) * RT)
        norm = jnp.sum(total[mine, :], axis=1, keepdims=True)
        some = norm > 0.0
        norm = jnp.where(some, norm, 1.0)
        mean = (latent[mine, :] / norm).astype(jnp.bfloat16)
        parts.append(dot(mean, wuv[h], ((1,), (0,))))
        logs.append(jnp.where(some, top[mine, 0:1] * SCALE + jnp.log(norm), NEG))
    diagonal = iota((96, 128), 0) == iota((96, 128), 1)
    which = iota((16, 128), 0)
    for z in range(NZ):
        rows = slice(z * RZ, (z + 1) * RZ)
        block = jnp.concatenate([part[rows] for part in parts], axis=0)
        out[z, 0:96, :] = block.astype(jnp.bfloat16)
        column = jnp.concatenate([log[rows] for log in logs], axis=0)
        row = jnp.sum(jnp.where(diagonal, column, 0.0), axis=0, keepdims=True)
        high_part = row.astype(jnp.bfloat16).astype(jnp.float32)
        middle = (row - high_part).astype(jnp.bfloat16).astype(jnp.float32)
        rest = row - high_part - middle
        packed = jnp.where(
            which == 0,
            high_part,
            jnp.where(which == 1, middle, jnp.where(which == 2, rest, 0.0)),
        )
        out[z, 96:112, :] = packed.astype(jnp.bfloat16)


def far_positions(pieces, lim, high, state):
    return pl.pallas_call(
        far_kernel,
        out_shape=jax.ShapeDtypeStruct((NZ, OUT_ROWS, 128), jnp.bfloat16),
        in_specs=[VMEM] * 10,
        out_specs=VMEM,
        scratch_shapes=[
            pltpu.VMEM((HG, C, DV), jnp.bfloat16),
            pltpu.VMEM((1, RH, S_DEV), jnp.float32),
            pltpu.VMEM((RH, 128), jnp.float32),
            pltpu.VMEM((RH, 128), jnp.float32),
            pltpu.VMEM((RH, C), jnp.float32),
        ],
        compiler_params=params(),
        cost_estimate=pl.CostEstimate(
            flops=2 * RH * (S_DEV * (2 * C + R) + DV * C),
            bytes_accessed=8 * 1024 * 1024,
            transcendentals=RH * S_DEV,
        ),
        name="far_positions",
    )(*pieces, lim, high, *state)


def combine_kernel(parts, *outs):
    logs = []
    for z in range(NZ):
        packed = parts[z, 96:112, :].astype(jnp.float32)
        logs.append(packed[0:1] + packed[1:2] + packed[2:3])
    best = functools.reduce(jnp.maximum, logs)
    shares = [jnp.exp(log - best) for log in logs]
    norm = functools.reduce(jnp.add, shares)
    diagonal = iota((96, 128), 0) == iota((96, 128), 1)
    summed = jnp.zeros((96, 128), jnp.float32)
    for z in range(NZ):
        share = jnp.where(diagonal, shares[z] / norm, 0.0)
        column = jnp.sum(share, axis=1, keepdims=True)
        summed += column * parts[z, 0:96, :].astype(jnp.float32)
    row = iota((128, 96), 0)
    which, rest = row >> 5, row & 31
    head = (rest * 43) >> 8
    source = jnp.where(rest < 24, head * 24 + (my_quad() ^ which) * 6 + rest - head * 6, -1)
    pick = jnp.where(source == iota((128, 96), 1), 1.0, 0.0).astype(jnp.bfloat16)
    rows = dot(pick, summed.astype(jnp.bfloat16), ((1,), (0,))).astype(jnp.bfloat16)
    for k in range(NQ):
        outs[k][...] = rows[32 * k : 32 * (k + 1)]


def combine(parts):
    return pl.pallas_call(
        combine_kernel,
        out_shape=(jax.ShapeDtypeStruct((32, 128), jnp.bfloat16),) * NQ,
        in_specs=[VMEM],
        out_specs=(VMEM,) * NQ,
        compiler_params=params(8),
        name="combine",
    )(parts)


def quad_swap(x, k):
    return lax.ppermute(x, ("x", "core"), [(i, i ^ k) for i in range(NQ)])


def z_shift(x, k):
    return lax.ppermute(x, "z", [(i, (i + k) % NZ) for i in range(NZ)])


def opposite(up2, down2):
    core = lax.axis_index("core")
    pairs = [
        (2 * i + c, 2 * ((i + (2 if c == 0 else -2)) % NZ) + c) for i in range(NZ) for c in range(2)
    ]
    return lax.ppermute(jnp.where(core == 0, up2, down2), ("z", "core"), pairs)


def by_sender(got):
    quad = my_quad()
    odd, upper = quad % 2 == 1, quad >= 2
    a, b, c, d = got
    a, b, c, d = (
        jnp.where(odd, b, a),
        jnp.where(odd, a, b),
        jnp.where(odd, d, c),
        jnp.where(odd, c, d),
    )
    return [
        jnp.where(upper, c, a),
        jnp.where(upper, d, b),
        jnp.where(upper, a, c),
        jnp.where(upper, b, d),
    ]


def body(queries, cache, w_uk, w_uv, selected, lengths):
    sent = prepare(queries, w_uk, w_uv)
    got = jnp.stack(by_sender([sent[0]] + [quad_swap(sent[k], k) for k in range(1, NQ)]))
    piece = jnp.concatenate(
        [
            got[:, 128:152].reshape(NQ, HG, 6, 128).transpose(1, 0, 2, 3).reshape(96, 128),
            got[:, 160:172].reshape(NQ, 2, 6, 128).transpose(1, 0, 2, 3).reshape(48, 128),
            got[:, 0:64].reshape(NQ, 16, 4, 128).transpose(1, 0, 2, 3).reshape(256, 128),
            got[:, 64:128].reshape(NQ, HG, 16, 128).transpose(1, 0, 2, 3).reshape(256, 128),
        ],
        axis=0,
    )
    lim = visible_limits(selected, lengths)
    piece, lim, cache = lax.optimization_barrier((piece, lim, cache.T))
    low, mate = quad_swap(cache, 2), quad_swap(cache, 1)
    up1, down1 = z_shift(piece, 1), z_shift(piece, -1)
    up2, down2 = z_shift(piece, 2), z_shift(piece, -2)
    mate, up1, down1, up2, down2 = lax.optimization_barrier((mate, up1, down1, up2, down2))
    up3, down3 = z_shift(up2, 1), z_shift(down2, -1)
    late = [up3, down3, opposite(up2, down2)]
    early, mate = settle([piece, up1, down1, up2, down2], mate)

    low, late = lax.optimization_barrier((low, late))
    high = quad_swap(low, 1)
    probe, *state = near_positions([early] + late, lim, cache, mate, low)
    parts = far_positions([early] + late, lim, high, (probe, *state))
    parts = lax.all_to_all(parts, "z", 0, 0, tiled=True)
    mine = combine(parts)
    got = [mine[0]] + [quad_swap(mine[k], k) for k in range(1, NQ)]
    final = jnp.stack(by_sender(got))[:, :24]
    final = final.reshape(NQ, HG, STEPS, 2, DV).transpose(2, 3, 0, 1, 4)
    return final.reshape(STEPS, 2, NQ * HG, DV)


def solution(mesh):
    fine = Mesh(mesh.devices.reshape(NZ, 2, 2, -1), ("z", "x", "core", "head"))
    ctx = ("z", "x", "core")
    in_specs = (
        P(None, ctx, "head", None),
        P(ctx, None),
        P("head", ctx, None),
        P("head", ctx, None),
        P(),
        P(),
    )
    out_specs = P(None, ctx, "head", None)
    return jax.shard_map(body, mesh=fine, in_specs=in_specs, out_specs=out_specs, check_vma=False)
```

```python
import functools

import jax
import jax.numpy as jnp
from jax import lax
from jax.experimental import pallas as pl
from jax.experimental.pallas import tpu as pltpu
from jax.sharding import Mesh
from jax.sharding import PartitionSpec as P

DN = 128
R = 64
C = 512
DV = 128
BLK = 128
STEPS = 3
TOPK = 16

NZ = 8
NQ = 4
HG = 4
BZ = 8
RZ = STEPS * BZ
RT = NZ * RZ
RH = HG * RT
S_DEV = 1024
NBLK = S_DEV // BLK

QN0, QR0, UK0, UV0, PIECE = 0, 96, 144, 400, 656
OFFSETS = (0, -1, 1, -2, 2, -3, 3, 4)
EARLY = 5
OUT_ROWS = 112

NEG = -1e30
SCALE = (DN + R) ** (-0.5)
LOG2E = 1.4426950408889634

VMEM = pl.BlockSpec(memory_space=pltpu.VMEM)
HBM = pl.BlockSpec(memory_space=pltpu.HBM)


def dot(a, b, dims):
    return lax.dot_general(a, b, (dims, ((), ())), preferred_element_type=jnp.float32)


def iota(shape, dim):
    return lax.broadcasted_iota(jnp.int32, shape, dim)


def params(mebibytes=24):
    return pltpu.CompilerParams(vmem_limit_bytes=mebibytes * 1024 * 1024)


def my_z():
    return lax.axis_index("z")


def my_quad():
    return lax.axis_index("x") * 2 + lax.axis_index("core")


def limits_kernel(chosen, lengths, out):
    z, quad = my_z(), my_quad()
    length = lengths[...]
    columns = [
        jnp.concatenate(
            [chosen[t], length >> 8, length & 255, jnp.zeros((14, 64), jnp.int32)], axis=0
        )
        for t in range(STEPS)
    ]
    table = jnp.concatenate(columns, axis=1).astype(jnp.float32).astype(jnp.bfloat16)
    row = iota((RT, RT), 0)
    row_z = (row * 2731) >> 16
    rest = row - row_z * RZ
    row_quad = (rest * 43) >> 8
    rest = rest - row_quad * 6
    source = (rest >> 1) * 64 + row_z * BZ + row_quad * 2 + (rest & 1)
    pick = jnp.where(source == iota((RT, RT), 1), 1.0, 0.0).astype(jnp.bfloat16)
    rows = dot(pick, table, ((1,), (1,))).astype(jnp.int32)
    row = iota((RT, 1), 0)
    within = row - ((row * 10923) >> 16) * 6
    ends = rows[:, 16:17] * 256 + rows[:, 17:18] + (within >> 1)
    lane = iota((RT, 128), 1)
    for i in range(NQ):
        block = (z * NQ + (quad ^ i)) * NBLK + lane
        hit = block == rows[:, 0:1]
        for k in range(1, TOPK):
            hit = jnp.logical_or(hit, block == rows[:, k : k + 1])
        count = jnp.clip(ends - block * BLK, 0, BLK)
        out[i] = jnp.where(hit, count, 0)


def visible_limits(selected, lengths):
    return pl.pallas_call(
        limits_kernel,
        out_shape=jax.ShapeDtypeStruct((NQ, RT, 128), jnp.int32),
        in_specs=[VMEM] * 2,
        out_specs=VMEM,
        name="limits",
    )(selected.transpose(0, 2, 1), lengths.reshape(1, -1))


def attend(parts, first, lim, probe, scores, top, total, latent, copies=()):
    lane = iota((RT, BLK), 1)
    old = top[...]
    for i, part in enumerate(parts):
        if i == len(parts) - 1:
            for copy in copies:
                copy.wait()
        whole = dot(probe[...], part[...], ((1,), (0,)))
        for h in range(HG):
            mine = slice(h * RT, (h + 1) * RT)
            best = top[mine, :]
            for j in range(NBLK):
                seen = lane < lim[first + i, :, j : j + 1]
                block = jnp.where(seen, whole[mine, j * BLK : (j + 1) * BLK], NEG)
                scores[i, mine, j * BLK : (j + 1) * BLK] = block
                best = jnp.maximum(best, block)
            top[mine, :] = best
    best = jnp.broadcast_to(jnp.max(top[...], axis=1, keepdims=True), top.shape)
    top[...] = best
    if first:
        fade = jnp.exp2((old - jnp.maximum(best, 0.1 * NEG)) * (SCALE * LOG2E))
        total[...] = total[...] * fade
        for c in range(C // 128):
            here = slice(c * 128, (c + 1) * 128)
            latent[:, here] = latent[:, here] * fade
    for i, part in enumerate(parts):
        weights = []
        for h in range(HG):
            mine = slice(h * RT, (h + 1) * RT)
            best = jnp.maximum(top[mine, :], 0.1 * NEG)
            summed = total[mine, :]
            blocks = []
            for j in range(NBLK):
                block = scores[i, mine, j * BLK : (j + 1) * BLK]
                weight = jnp.exp2((block - best) * (SCALE * LOG2E))
                summed = summed + weight
                blocks.append(weight.astype(jnp.bfloat16))
            total[mine, :] = summed
            weights.append(jnp.concatenate(blocks, axis=1))
        latent[...] += dot(jnp.concatenate(weights, axis=0), part[0:C, :], ((1,), (1,)))


def prepare_kernel(queries, keys, values, *refs):
    outs, (q, uk, uv, sems) = refs[:NQ], refs[NQ:]
    copies = [
        pltpu.make_async_copy(source, target, sems.at[i])
        for i, (source, target) in enumerate(((queries, q), (keys, uk), (values, uv)))
    ]
    for copy in copies:
        copy.start()
    quad = my_quad()
    row = iota((128, 96), 0)
    rest = row & 31
    head = (rest * 43) >> 8
    source = (rest - head * 6) * 16 + (quad ^ (row >> 5)) * HG + head
    source = jnp.where(rest < 24, source, -1)
    pick = jnp.where(source == iota((128, 96), 1), 1.0, 0.0).astype(jnp.bfloat16)
    row = iota((64, 96), 0)
    rest = row & 15
    pair = jnp.where(rest < 6, 0, 1)
    source = (rest - pair * 6) * 16 + (quad ^ (row >> 4)) * HG + pair * 2
    source = jnp.where(rest < 12, source, -1)
    column = iota((64, 96), 1)
    pick_even = jnp.where(source == column, 1.0, 0.0).astype(jnp.bfloat16)
    pick_odd = jnp.where(source == column - 1, 1.0, 0.0).astype(jnp.bfloat16)
    pick_odd = jnp.where(rest < 12, pick_odd, 0.0).astype(jnp.bfloat16)
    row = iota((64, 64), 0)
    source = (quad ^ (row >> 4)) * 16 + (row & 15)
    pick_keys = jnp.where(source == iota((64, 64), 1), 1.0, 0.0).astype(jnp.bfloat16)
    copies[0].wait()
    table = q[...].reshape(96, DN + R)
    plain = dot(pick, table[:, :DN], ((1,), (0,))).astype(jnp.bfloat16)
    rope = table[:, DN:]
    rope = jnp.concatenate(
        [dot(pick_even, rope, ((1,), (0,))), dot(pick_odd, rope, ((1,), (0,)))], axis=1
    ).astype(jnp.bfloat16)
    copies[1].wait()
    table = uk[...].astype(jnp.float32).reshape(64, C).astype(jnp.bfloat16)
    table = dot(pick_keys, table, ((1,), (0,))).astype(jnp.bfloat16)
    copies[2].wait()
    for k in range(NQ):
        for cc in range(4):
            outs[k][cc * 16 : (cc + 1) * 16, :] = table[
                k * 16 : (k + 1) * 16, cc * 128 : (cc + 1) * 128
            ]
        for h in range(HG):
            outs[k][64 + h * 16 : 80 + h * 16, :] = uv[(quad ^ k) * HG + h]
        outs[k][128:160, :] = plain[k * 32 : (k + 1) * 32]
        outs[k][160:176, :] = rope[k * 16 : (k + 1) * 16]


def prepare(queries, w_uk, w_uv):
    return pl.pallas_call(
        prepare_kernel,
        out_shape=(jax.ShapeDtypeStruct((176, 128), jnp.bfloat16),) * NQ,
        in_specs=[HBM] * 3,
        out_specs=(VMEM,) * NQ,
        scratch_shapes=[
            pltpu.VMEM((STEPS * 2, 16, DN + R), jnp.bfloat16),
            pltpu.VMEM((16, 4, C), jnp.bfloat16),
            pltpu.VMEM((16, 16, DV), jnp.bfloat16),
            pltpu.SemaphoreType.DMA((3,)),
        ],
        compiler_params=params(60),
        name="prepare",
    )(queries.reshape(STEPS * 2, 16, DN + R), w_uk, w_uv)


def settle_kernel(*refs):
    arrived, mate_in, pieces, mate = refs[:EARLY], refs[EARLY], refs[EARLY + 1], refs[EARLY + 2]
    for p in range(EARLY):
        pieces[p] = arrived[p][...]
    mate[...] = mate_in[...]


def settle(arrived, mate):
    return pl.pallas_call(
        settle_kernel,
        out_shape=(
            jax.ShapeDtypeStruct((EARLY, PIECE, 128), jnp.bfloat16),
            jax.ShapeDtypeStruct(mate.shape, mate.dtype),
        ),
        in_specs=[VMEM] * (EARLY + 1),
        out_specs=(VMEM,) * 2,
        compiler_params=params(8),
        name="settle",
    )(*arrived, mate)


def near_kernel(*refs):
    early, late, (lim, own, mate, low) = refs[0], refs[1:4], refs[4:8]
    probe, top, total, latent, qn, qr, wuk, scores, other, sem = refs[8:]
    copy = pltpu.make_async_copy(low, other, sem)
    copy.start()
    pieces = [early.at[p] for p in range(EARLY)] + list(late)
    for p, offset in enumerate(OFFSETS):
        z = (my_z() + offset) & (NZ - 1)
        here = pl.ds(pl.multiple_of(z * RZ, RZ), RZ)
        block = pieces[p][QN0 : QN0 + 96, :].astype(jnp.float32)
        for h in range(HG):
            qn[h, here, :] = block[h * RZ : (h + 1) * RZ]
        block = pieces[p][QR0 : QR0 + 48, :].astype(jnp.float32)
        for j in range(HG // 2):
            qr[j, here, :] = block[j * RZ : (j + 1) * RZ]
        here = pl.ds(pl.multiple_of(z * 16, 16), 16)
        for h in range(HG):
            for cc in range(4):
                first = UK0 + (cc * HG + h) * 16
                wuk[h, here, cc * 128 : (cc + 1) * 128] = pieces[p][first : first + 16, :]
    for h in range(HG):
        mine = slice(h * RT, (h + 1) * RT)
        absorbed = dot(qn[h].astype(jnp.bfloat16), wuk[h], ((1,), (0,)))
        probe[mine, 0:C] = absorbed.astype(jnp.bfloat16)
        rope = qr[h // 2][:, (h % 2) * R : (h % 2 + 1) * R]
        probe[mine, C : C + R] = rope.astype(jnp.bfloat16)
    top[...] = jnp.full(top.shape, NEG, jnp.float32)
    total[...] = jnp.zeros(total.shape, jnp.float32)
    latent[...] = jnp.zeros(latent.shape, jnp.float32)
    attend((own, mate, other), 0, lim, probe, scores, top, total, latent, (copy,))


def near_positions(pieces, lim, own, mate, low):
    return pl.pallas_call(
        near_kernel,
        out_shape=(
            jax.ShapeDtypeStruct((RH, C + R), jnp.bfloat16),
            jax.ShapeDtypeStruct((RH, 128), jnp.float32),
            jax.ShapeDtypeStruct((RH, 128), jnp.float32),
            jax.ShapeDtypeStruct((RH, C), jnp.float32),
        ),
        in_specs=[VMEM] * 7 + [HBM],
        out_specs=(VMEM,) * 4,
        scratch_shapes=[
            pltpu.VMEM((HG, RT, DN), jnp.float32),
            pltpu.VMEM((HG // 2, RT, 2 * R), jnp.float32),
            pltpu.VMEM((HG, DN, C), jnp.bfloat16),
            pltpu.VMEM((3, RH, S_DEV), jnp.float32),
            pltpu.VMEM((C + R, S_DEV), jnp.bfloat16),
            pltpu.SemaphoreType.DMA(()),
        ],
        compiler_params=params(),
        cost_estimate=pl.CostEstimate(
            flops=2 * RH * (3 * S_DEV * (2 * C + R) + DN * C),
            bytes_accessed=8 * 1024 * 1024,
            transcendentals=RH * 3 * S_DEV,
        ),
        name="near_positions",
    )(*pieces, lim, own, mate, low)


def far_kernel(*refs):
    early, late, (lim, high, probe, top_in, total_in, latent_in) = refs[0], refs[1:4], refs[4:10]
    out, wuv, scores, top, total, latent = refs[10:]
    pieces = [early.at[p] for p in range(EARLY)] + list(late)
    for p, offset in enumerate(OFFSETS):
        z = (my_z() + offset) & (NZ - 1)
        here = pl.ds(pl.multiple_of(z * 64, 64), 64)
        for h in range(HG):
            wuv[h, here, :] = pieces[p][UV0 + h * 64 : UV0 + (h + 1) * 64, :]
    top[...] = top_in[...]
    total[...] = total_in[...]
    latent[...] = latent_in[...]
    attend((high,), 3, lim, probe, scores, top, total, latent)

    parts, logs = [], []
    for h in range(HG):
        mine = slice(h * RT, (h + 1) * RT)
        norm = jnp.sum(total[mine, :], axis=1, keepdims=True)
        some = norm > 0.0
        norm = jnp.where(some, norm, 1.0)
        mean = (latent[mine, :] / norm).astype(jnp.bfloat16)
        parts.append(dot(mean, wuv[h], ((1,), (0,))))
        logs.append(jnp.where(some, top[mine, 0:1] * SCALE + jnp.log(norm), NEG))
    diagonal = iota((96, 128), 0) == iota((96, 128), 1)
    which = iota((16, 128), 0)
    for z in range(NZ):
        rows = slice(z * RZ, (z + 1) * RZ)
        block = jnp.concatenate([part[rows] for part in parts], axis=0)
        out[z, 0:96, :] = block.astype(jnp.bfloat16)
        column = jnp.concatenate([log[rows] for log in logs], axis=0)
        row = jnp.sum(jnp.where(diagonal, column, 0.0), axis=0, keepdims=True)
        high_part = row.astype(jnp.bfloat16).astype(jnp.float32)
        middle = (row - high_part).astype(jnp.bfloat16).astype(jnp.float32)
        rest = row - high_part - middle
        packed = jnp.where(
            which == 0,
            high_part,
            jnp.where(which == 1, middle, jnp.where(which == 2, rest, 0.0)),
        )
        out[z, 96:112, :] = packed.astype(jnp.bfloat16)


def far_positions(pieces, lim, high, state):
    return pl.pallas_call(
        far_kernel,
        out_shape=jax.ShapeDtypeStruct((NZ, OUT_ROWS, 128), jnp.bfloat16),
        in_specs=[VMEM] * 10,
        out_specs=VMEM,
        scratch_shapes=[
            pltpu.VMEM((HG, C, DV), jnp.bfloat16),
            pltpu.VMEM((1, RH, S_DEV), jnp.float32),
            pltpu.VMEM((RH, 128), jnp.float32),
            pltpu.VMEM((RH, 128), jnp.float32),
            pltpu.VMEM((RH, C), jnp.float32),
        ],
        compiler_params=params(),
        cost_estimate=pl.CostEstimate(
            flops=2 * RH * (S_DEV * (2 * C + R) + DV * C),
            bytes_accessed=8 * 1024 * 1024,
            transcendentals=RH * S_DEV,
        ),
        name="far_positions",
    )(*pieces, lim, high, *state)


def combine_kernel(parts, *outs):
    logs = []
    for z in range(NZ):
        packed = parts[z, 96:112, :].astype(jnp.float32)
        logs.append(packed[0:1] + packed[1:2] + packed[2:3])
    best = functools.reduce(jnp.maximum, logs)
    shares = [jnp.exp(log - best) for log in logs]
    norm = functools.reduce(jnp.add, shares)
    diagonal = iota((96, 128), 0) == iota((96, 128), 1)
    summed = jnp.zeros((96, 128), jnp.float32)
    for z in range(NZ):
        share = jnp.where(diagonal, shares[z] / norm, 0.0)
        column = jnp.sum(share, axis=1, keepdims=True)
        summed += column * parts[z, 0:96, :].astype(jnp.float32)
    row = iota((128, 96), 0)
    which, rest = row >> 5, row & 31
    head = (rest * 43) >> 8
    source = jnp.where(rest < 24, head * 24 + (my_quad() ^ which) * 6 + rest - head * 6, -1)
    pick = jnp.where(source == iota((128, 96), 1), 1.0, 0.0).astype(jnp.bfloat16)
    rows = dot(pick, summed.astype(jnp.bfloat16), ((1,), (0,))).astype(jnp.bfloat16)
    for k in range(NQ):
        outs[k][...] = rows[32 * k : 32 * (k + 1)]


def combine(parts):
    return pl.pallas_call(
        combine_kernel,
        out_shape=(jax.ShapeDtypeStruct((32, 128), jnp.bfloat16),) * NQ,
        in_specs=[VMEM],
        out_specs=(VMEM,) * NQ,
        compiler_params=params(8),
        name="combine",
    )(parts)


def quad_swap(x, k):
    return lax.ppermute(x, ("x", "core"), [(i, i ^ k) for i in range(NQ)])


def z_shift(x, k):
    return lax.ppermute(x, "z", [(i, (i + k) % NZ) for i in range(NZ)])


def opposite(up2, down2):
    core = lax.axis_index("core")
    pairs = [
        (2 * i + c, 2 * ((i + (2 if c == 0 else -2)) % NZ) + c) for i in range(NZ) for c in range(2)
    ]
    return lax.ppermute(jnp.where(core == 0, up2, down2), ("z", "core"), pairs)


def by_sender(got):
    quad = my_quad()
    odd, upper = quad % 2 == 1, quad >= 2
    a, b, c, d = got
    a, b, c, d = (
        jnp.where(odd, b, a),
        jnp.where(odd, a, b),
        jnp.where(odd, d, c),
        jnp.where(odd, c, d),
    )
    return [
        jnp.where(upper, c, a),
        jnp.where(upper, d, b),
        jnp.where(upper, a, c),
        jnp.where(upper, b, d),
    ]


def body(queries, cache, w_uk, w_uv, selected, lengths):
    sent = prepare(queries, w_uk, w_uv)
    got = jnp.stack(by_sender([sent[0]] + [quad_swap(sent[k], k) for k in range(1, NQ)]))
    piece = jnp.concatenate(
        [
            got[:, 128:152].reshape(NQ, HG, 6, 128).transpose(1, 0, 2, 3).reshape(96, 128),
            got[:, 160:172].reshape(NQ, 2, 6, 128).transpose(1, 0, 2, 3).reshape(48, 128),
            got[:, 0:64].reshape(NQ, 16, 4, 128).transpose(1, 0, 2, 3).reshape(256, 128),
            got[:, 64:128].reshape(NQ, HG, 16, 128).transpose(1, 0, 2, 3).reshape(256, 128),
        ],
        axis=0,
    )
    lim = visible_limits(selected, lengths)
    piece, cache = lax.optimization_barrier((piece, cache.T))
    low, mate = quad_swap(cache, 2), quad_swap(cache, 1)
    up1, down1 = z_shift(piece, 1), z_shift(piece, -1)
    up2, down2 = z_shift(piece, 2), z_shift(piece, -2)
    mate, up1, down1, up2, down2 = lax.optimization_barrier((mate, up1, down1, up2, down2))
    up3, down3 = z_shift(up2, 1), z_shift(down2, -1)
    late = [up3, down3, opposite(up2, down2)]
    early, mate = settle([piece, up1, down1, up2, down2], mate)

    low, late = lax.optimization_barrier((low, late))
    high = quad_swap(low, 1)
    probe, *state = near_positions([early] + late, lim, cache, mate, low)
    parts = far_positions([early] + late, lim, high, (probe, *state))
    parts = lax.all_to_all(parts, "z", 0, 0, tiled=True)
    mine = combine(parts)
    got = [mine[0]] + [quad_swap(mine[k], k) for k in range(1, NQ)]
    final = jnp.stack(by_sender(got))[:, :24]
    final = final.reshape(NQ, HG, STEPS, 2, DV).transpose(2, 3, 0, 1, 4)
    return final.reshape(STEPS, 2, NQ * HG, DV)


def solution(mesh):
    fine = Mesh(mesh.devices.reshape(NZ, 2, 2, -1), ("z", "x", "core", "head"))
    ctx = ("z", "x", "core")
    in_specs = (
        P(None, ctx, "head", None),
        P(ctx, None),
        P("head", ctx, None),
        P("head", ctx, None),
        P(),
        P(),
    )
    out_specs = P(None, ctx, "head", None)
    return jax.shard_map(body, mesh=fine, in_specs=in_specs, out_specs=out_specs, check_vma=False)
```
